32 devices in a mesh: tm: 4 (over z), tensor: 8 (over y, x, core).
Axes of the slice: x: 2, y: 2, z: 4, core: 2. Of those that a mesh axis runs over, the one named last changes fastest.
Arguments:
- integrals: bfloat16 [1024, 2, 4096], P('tensor'), may hold values from -0.75 to 0.75
- pair_lists: int32 [16, 2], replicated, may hold values from 0 to 7, as said below
- occ_density: bfloat16 [4, 8, 64, 64], P('tm', 'tensor'), may hold values from -0.75 to 0.75
- virt_density: bfloat16 [4, 8, 64, 64], P('tm', 'tensor'), may hold values from -0.75 to 0.75
- cosine_weights: float32 [4, 4], replicated, may hold values from -3 to 3
- coulomb_blocks: float32 [16, 64, 64], replicated, may hold values from -0.75 to 0.75
Outputs:
- screened: float32 [4, 1024, 1024], P('tm', 'tensor')
The draws below stay inside these ranges and needn't reach their ends.
Inputs may be any that keep to these rules, and one draw needn't show every extreme that they name: `pair_lists`: row p names the 2 pair blocks listed with aux block p, all different, in ascending order. Every pair block is named in 1 to 6 rows, and some pair block in exactly 6 rows.
All inputs are finite; a program needn't handle non-finite values.
Results may differ from the reference program's by a relative error of at most 0.01.
Values may be sent and summed in bfloat16 or wider, within the bound.
No kernel may reach another device: no remote copies, remote signals or barrier semaphores. Data moves between devices by JAX's collectives and lax.ppermute only.
A program may use at most 64 MiB of HBM per device.

```python
import jax
import jax.numpy as jnp
from jax import lax

SLAB = 1024
AUXB = 64
ORB = 64
MOST = 6
TIMES = 4
FREQS = 4
PB = 16
PAIRS = 8
CAPS = 2


def draw_pair_lists(key, part):
    key_order = jax.random.fold_in(key, 11)
    key_caps = jax.random.fold_in(key, 23)
    key_label = jax.random.fold_in(key, 37)
    order = jax.random.permutation(key_order, PAIRS).astype(jnp.int32)
    removable = jax.random.randint(key_caps, (PAIRS,), 3, MOST, dtype=jnp.int32)
    removable = removable.at[0].set(0)
    excess = PAIRS * MOST - PB * CAPS
    before = jnp.cumsum(removable) - removable
    removed = jnp.clip(excess - before, 0, removable)
    counts = jnp.zeros((PAIRS,), jnp.int32).at[order].set(MOST - removed)
    ends = jnp.cumsum(counts)
    slot_ids = jnp.arange(PB * CAPS, dtype=jnp.int32)
    owners = jnp.sum((ends[None, :] <= slot_ids[:, None]).astype(jnp.int32), axis=1)
    table = owners.reshape(CAPS, PB).T
    relabel = jax.random.permutation(key_label, PB)
    return table[relabel].astype(jnp.int32)


def block_scale(rng, shape, shards, smallest, high):
    def one(axis_at, parts):
        steps = jax.random.uniform(jax.random.fold_in(jax.random.fold_in(rng, 6), axis_at), (parts,), jnp.float32, smallest / len(shards), high / len(shards))
        return jnp.repeat(jnp.exp(steps), shape[axis_at] // parts).reshape((-1,) + (1,) * (len(shape) - axis_at - 1))

    level = one(*shards[0])
    for cut in shards[1:]:
        level = level * one(*cut)
    return level


def gaussian(stream_key, shape, scale, bound, cuts=(), kind=jnp.bfloat16):
    loudness = block_scale(stream_key, shape, cuts, -0.22, 0.18) if cuts else 1.0
    array = jax.random.normal(stream_key, shape, jnp.float32) * scale * loudness
    return jnp.minimum(jnp.maximum(array, -bound), bound).astype(kind)


def setup_inputs(seed: int = 0) -> dict:
    seeds = jax.random.split(jax.random.key(seed), 7)
    integrals = gaussian(seeds[0], (SLAB, CAPS, ORB * ORB), 0.125, 0.75, ((0, 8),))
    pair_lists = draw_pair_lists(jax.random.fold_in(seeds[6], 71), 0)
    occ_density = gaussian(seeds[2], (TIMES, PAIRS, ORB, ORB), ORB ** -0.5, 0.75, ((0, 4), (1, 8)))
    virt_density = gaussian(seeds[3], (TIMES, PAIRS, ORB, ORB), ORB ** -0.5, 0.75, ((0, 4), (1, 8)))
    cosine_weights = gaussian(seeds[4], (FREQS, TIMES), TIMES ** -0.5, 3.0, (), jnp.float32)
    coulomb_blocks = gaussian(seeds[5], (PB, AUXB, AUXB), AUXB ** -0.5, 0.75, (), jnp.float32)
    return dict(integrals=integrals, pair_lists=pair_lists, occ_density=occ_density, virt_density=virt_density, cosine_weights=cosine_weights, coulomb_blocks=coulomb_blocks)


def listed_blocks(pair_lists, pair_index):
    block_count = pair_lists.shape[0]
    member = jnp.any(pair_lists == pair_index, axis=1)
    positions = jnp.cumsum(member.astype(jnp.int32)) - 1
    slot_ids = jnp.arange(MOST, dtype=jnp.int32)
    matches = member[None, :] & (positions[None, :] == slot_ids[:, None])
    labels = jnp.arange(block_count, dtype=jnp.int32)
    located = jnp.sum(jnp.where(matches, labels[None, :], 0), axis=1).astype(jnp.int32)
    return jnp.where(jnp.any(matches, axis=1), located, block_count).astype(jnp.int32)


def density_product(row_data, occupied, virtual):
    row_count = row_data.shape[0]
    orbital_width = occupied.shape[0]
    half_done = jnp.dot(row_data.reshape(row_count * orbital_width, orbital_width), virtual, preferred_element_type=jnp.float32)
    half_done = half_done.astype(jnp.bfloat16).reshape(row_count, orbital_width, orbital_width)
    contracted = jnp.einsum("rms,ml->rls", half_done.astype(jnp.float32), occupied.astype(jnp.float32))
    return contracted.astype(jnp.bfloat16).reshape(row_count, orbital_width * orbital_width)


def pair_column(integrals, pair_lists, pair_index):
    row_block = jnp.arange(SLAB, dtype=jnp.int32) // AUXB
    chosen = pair_lists[row_block] == pair_index
    list_pos = jnp.sum(jnp.where(chosen, jnp.arange(CAPS, dtype=jnp.int32)[None, :], 0), axis=1).astype(jnp.int32)
    picked = jnp.take_along_axis(integrals, list_pos[:, None, None], axis=1)[:, 0]
    return jnp.where(jnp.any(chosen, axis=1)[:, None], picked, jnp.zeros_like(picked))


def reference(integrals, pair_lists, occ_density, virt_density, cosine_weights, coulomb_blocks):
    pair_ids = jnp.arange(PAIRS, dtype=jnp.int32)

    def one_time(time_step):
        def one_pair(chi_sum, pair_index):
            column = pair_column(integrals, pair_lists, pair_index)
            chosen = listed_blocks(pair_lists, pair_index)
            wanted = (chosen[:, None] * AUXB + jnp.arange(AUXB, dtype=jnp.int32)[None, :]).reshape(-1)
            tile_rows = jnp.take(column, wanted, axis=0, mode="fill", fill_value=0)
            weighted = density_product(tile_rows, occ_density[time_step, pair_index], virt_density[time_step, pair_index])
            gram_block = jnp.dot(weighted, tile_rows.T, preferred_element_type=jnp.float32)
            rounded = lax.optimization_barrier(gram_block.astype(jnp.bfloat16)).astype(jnp.float32)
            squares = rounded.reshape(MOST, AUXB, MOST, AUXB).transpose(0, 2, 1, 3)
            chi_sum = chi_sum.at[chosen[:, None], :, chosen[None, :], :].add(squares, mode="drop")
            return chi_sum, None

        start_sum = jnp.zeros((PB, AUXB, PB, AUXB), jnp.float32)
        chi_sum, unused = lax.scan(one_pair, start_sum, pair_ids)
        return chi_sum.reshape(SLAB, SLAB)

    chi_time = lax.map(one_time, jnp.arange(TIMES, dtype=jnp.int32))
    chi_freq = jnp.einsum("ft,tab->fab", cosine_weights, chi_time, precision=lax.Precision.HIGHEST)
    shaped = chi_freq.reshape(FREQS, SLAB, PB, AUXB)
    screened = jnp.einsum("frpa,pab->frpb", shaped, coulomb_blocks, precision=lax.Precision.HIGHEST)
    return screened.reshape(FREQS, SLAB, SLAB)
```

```python
import functools

import jax
import jax.numpy as jnp
from jax import lax
from jax.experimental import pallas as pl
from jax.experimental.pallas import tpu as pltpu
from jax.sharding import PartitionSpec as P

MOST = 6
HALF = 64
LANES = 128


def listed_blocks(pair_lists, pair_index):
    block_count = pair_lists.shape[0]
    member = jnp.any(pair_lists == pair_index, axis=1)
    positions = jnp.cumsum(member.astype(jnp.int32)) - 1
    slot_ids = jnp.arange(MOST, dtype=jnp.int32)
    matches = member[None, :] & (positions[None, :] == slot_ids[:, None])
    labels = jnp.arange(block_count, dtype=jnp.int32)
    located = jnp.sum(jnp.where(matches, labels[None, :], 0), axis=1)
    return jnp.where(jnp.any(matches, axis=1), located, block_count)


def density_product(row_data, occupied, virtual):
    row_count = row_data.shape[0]
    orbital_width = occupied.shape[0]
    half_done = jnp.dot(
        row_data.reshape(row_count * orbital_width, orbital_width),
        virtual,
        preferred_element_type=jnp.float32,
    )
    half_done = half_done.astype(jnp.bfloat16).reshape(row_count, orbital_width, orbital_width)
    contracted = jnp.einsum("rms,ml->rls", half_done, occupied, preferred_element_type=jnp.float32)
    return contracted.astype(jnp.bfloat16).reshape(row_count, orbital_width * orbital_width)


def pack_rows(local_rows, first_row, pair_lists, pair_count, block_rows):
    row_count = local_rows.shape[0]
    row_ids = first_row + jnp.arange(row_count, dtype=jnp.int32)
    targets = pair_lists[row_ids // block_rows]
    places = jnp.broadcast_to(jnp.arange(row_count, dtype=jnp.int32)[:, None], targets.shape)
    zero_buffer = jnp.zeros((pair_count, row_count, local_rows.shape[2]), local_rows.dtype)
    filled = zero_buffer.at[targets, places].set(local_rows)
    return filled.reshape(pair_count * row_count, local_rows.shape[2])


def any_slice(integrals, pair_lists, occ_density, virt_density, cosine_weights, coulomb_blocks):
    tensor_size = lax.axis_size("tensor")
    owner_pair = lax.axis_index("tensor")
    local_count = integrals.shape[0]
    slab_rows = local_count * tensor_size
    block_count = coulomb_blocks.shape[0]
    block_rows = coulomb_blocks.shape[1]
    occupied = occ_density[0, 0]
    virtual = virt_density[0, 0]
    chosen = listed_blocks(pair_lists, owner_pair)
    wanted = (
        chosen[:, None] * block_rows + jnp.arange(block_rows, dtype=jnp.int32)[None, :]
    ).reshape(-1)
    outgoing = pack_rows(integrals, owner_pair * local_count, pair_lists, tensor_size, block_rows)
    arrived = lax.all_to_all(outgoing, "tensor", split_axis=0, concat_axis=0, tiled=True)
    tile_rows = jnp.take(arrived, wanted, axis=0, mode="fill", fill_value=0)
    weighted = density_product(tile_rows, occupied, virtual)
    gram_block = lax.dot_general(
        weighted, tile_rows, (((1,), (1,)), ((), ())), preferred_element_type=jnp.float32
    )
    most_count = chosen.shape[0]
    block_ids = jnp.arange(block_count, dtype=jnp.int32)
    slot_ids = jnp.arange(most_count, dtype=jnp.int32)
    block_match = chosen[None, :] == block_ids[:, None]
    slot_of = jnp.sum(jnp.where(block_match, slot_ids[None, :], 0), axis=1)
    present = jnp.any(block_match, axis=1)
    slab_ids = jnp.arange(slab_rows, dtype=jnp.int32)
    row_block = slab_ids // block_rows
    source_row = jnp.where(
        present[row_block],
        slot_of[row_block] * block_rows + slab_ids % block_rows,
        most_count * block_rows,
    )
    rounded_terms = gram_block.astype(jnp.bfloat16)
    outgoing_terms = jnp.take(rounded_terms, source_row, axis=0, mode="fill", fill_value=0)
    arrived_terms = lax.all_to_all(
        outgoing_terms, "tensor", split_axis=0, concat_axis=0, tiled=True
    )
    received = arrived_terms.reshape(tensor_size, local_count, most_count, block_rows)
    every_chosen = jax.vmap(lambda pair_index: listed_blocks(pair_lists, pair_index))(
        jnp.arange(tensor_size, dtype=jnp.int32)
    )
    placement = (every_chosen[:, :, None] == block_ids[None, None, :]).astype(jnp.bfloat16)
    placed = jnp.einsum("srja,sjp->rpa", received, placement, preferred_element_type=jnp.float32)
    chi_rows = placed.reshape(local_count, slab_rows)
    spread = jnp.einsum(
        "ft,trc->frc",
        cosine_weights,
        lax.all_to_all(
            chi_rows[None].astype(jnp.bfloat16), "tm", split_axis=2, concat_axis=0, tiled=True
        ).astype(jnp.float32),
        precision=lax.Precision.HIGHEST,
    )
    freq_rows = lax.all_to_all(
        spread.astype(jnp.bfloat16), "tm", split_axis=0, concat_axis=2, tiled=True
    ).astype(spread.dtype)
    shaped = freq_rows.reshape(1, local_count, block_count, block_rows)
    screened = jnp.einsum("frpa,pab->frpb", shaped, coulomb_blocks, precision=lax.Precision.HIGHEST)
    return screened.reshape(1, local_count, slab_rows)


def swap_groups(rows_ref, out_ref):
    count = rows_ref.shape[0] // HALF
    left = lax.broadcasted_iota(jnp.int32, (count, LANES), 1) < HALF
    for pair in range(HALF // 2):
        even = rows_ref[pl.ds(2 * pair, count, stride=HALF), :]
        odd = rows_ref[pl.ds(2 * pair + 1, count, stride=HALF), :]
        first = jnp.where(left, even, pltpu.roll(odd, HALF, 1))
        second = jnp.where(left, pltpu.roll(even, HALF, 1), odd)
        out_ref[0, 0, :count, pair * LANES : (pair + 1) * LANES] = first.astype(out_ref.dtype)
        out_ref[0, 0, count:, pair * LANES : (pair + 1) * LANES] = second.astype(out_ref.dtype)


def turn_kernel(tile_ref, out_ref, rows_ref):
    count = rows_ref.shape[0] // HALF
    for piece in range(count):
        chunk = tile_ref[0, 0, :, piece * LANES : (piece + 1) * LANES]
        rows_ref[piece * HALF : (piece + 1) * HALF, :] = chunk.astype(jnp.float32)
    left = lax.broadcasted_iota(jnp.int32, (count, LANES), 1) < HALF
    for low in range(HALF // 2):
        near = rows_ref[pl.ds(low, count, stride=HALF), :]
        far = rows_ref[pl.ds(low + HALF // 2, count, stride=HALF), :]
        first = jnp.where(left, near, pltpu.roll(far, HALF, 1))
        second = jnp.where(left, pltpu.roll(near, HALF, 1), far)
        out_ref[0, 0, :count, low * LANES : (low + 1) * LANES] = first.astype(out_ref.dtype)
        out_ref[0, 0, count:, low * LANES : (low + 1) * LANES] = second.astype(out_ref.dtype)


def mix_kernel(turned_ref, density_ref, out_ref, rows_ref):
    occupied = density_ref[0, 0, :, :HALF]
    virtual = density_ref[0, 0, :, HALF:].astype(jnp.float32)
    wide = 4 * HALF
    row_ids = lax.broadcasted_iota(jnp.int32, (wide, wide), 0) // HALF
    col_ids = lax.broadcasted_iota(jnp.int32, (wide, wide), 1) // HALF
    twice = jnp.concatenate([virtual, virtual], axis=1)
    strip = jnp.concatenate([twice, twice], axis=1)
    tiled = jnp.concatenate([strip, strip, strip, strip], axis=0)
    diagonal = jnp.where(row_ids == col_ids, tiled, 0.0).astype(jnp.bfloat16)
    groups = turned_ref.shape[3] // wide
    halves = []
    for group in range(groups):
        half_done = jnp.dot(
            occupied,
            turned_ref[0, 0, :, group * wide : (group + 1) * wide],
            preferred_element_type=jnp.float32,
        )
        halves.append(half_done.astype(jnp.bfloat16))
    mixed = jnp.dot(
        jnp.concatenate(halves, axis=0), diagonal, preferred_element_type=jnp.float32
    )
    for group in range(groups):
        block = mixed[group * HALF : (group + 1) * HALF]
        rows_ref[2 * group * HALF : (2 * group + 1) * HALF, :] = block[:, :LANES]
        rows_ref[(2 * group + 1) * HALF : (2 * group + 2) * HALF, :] = block[:, LANES:]
    swap_groups(rows_ref, out_ref)


def gram_kernel(weights_ref, match_ref, *refs):
    mixed_refs, piece_refs = refs[:4], refs[4:12]
    out_ref, sum_ref = refs[12], refs[13]
    step = pl.program_id(0)
    caps = sum_ref.shape[0]

    @pl.when(step == 0)
    def _():
        sum_ref[...] = jnp.zeros_like(sum_ref)

    depth = mixed_refs[0].shape[-1]
    for column in range(caps):
        right = jnp.concatenate([piece[column] for piece in piece_refs], axis=0)
        for time in range(4):
            left = mixed_refs[time][...].reshape(-1, depth)
            sum_ref[column, time] += lax.dot_general(
                left, right, (((1,), (1,)), ((), ())), preferred_element_type=jnp.float32
            )

    @pl.when(step == pl.num_programs(0) - 1)
    def _():
        rows = out_ref.shape[1]
        for part in range(rows // HALF):
            chi = []
            for time in range(4):
                total = None
                for mine in range(caps):
                    place = mine * rows + part * HALF
                    for column in range(caps):
                        row = (mine * 2 + part) * caps + column
                        term = sum_ref[column, time, place : place + HALF, :] * match_ref[row : row + 1, :]
                        total = term if total is None else total + term
                chi.append(total)
            for freq in range(4):
                value = weights_ref[freq, 0] * chi[0]
                for time in range(1, 4):
                    value = value + weights_ref[freq, time] * chi[time]
                out_ref[freq, part * HALF : (part + 1) * HALF, :] = value.astype(out_ref.dtype)


def screen_kernel(place_ref, r0, r1, r2, r3, high_ref, low_ref, out_ref):
    plane, device = place_ref[0], place_ref[1]
    share = r0.shape[1] // 8
    for move in range(8):
        owner = device ^ move
        total = None
        for slot, ref in enumerate((r0, r1, r2, r3)):
            first = pl.multiple_of((plane ^ slot) * share, share)
            left = ref[:, move * share : (move + 1) * share]
            for factor in (high_ref, low_ref):
                term = jnp.dot(
                    left, factor[owner, pl.ds(first, share), :], preferred_element_type=jnp.float32
                )
                total = term if total is None else total + term
        out_ref[0, :, pl.ds(pl.multiple_of(owner * LANES, LANES), LANES)] = total


def small_slice(integrals, pair_lists, occ_density, virt_density, cosine_weights, coulomb_blocks):
    plane = lax.axis_index("tm")
    device = lax.axis_index("tensor")
    local_count, caps, pair_width = integrals.shape
    share = local_count // 4
    vmem = pl.BlockSpec(memory_space=pltpu.VMEM)
    smem = pl.BlockSpec(memory_space=pltpu.SMEM)
    params = pltpu.CompilerParams(vmem_limit_bytes=48 * 1024 * 1024)

    def across(array, move):
        return lax.ppermute(array, "tensor", [(i, i ^ move) for i in range(8)])

    def planes(array, move):
        return lax.ppermute(array, "tm", [(i, i ^ move) for i in range(4)])

    occupied = occ_density[0, 0].T.reshape(HALF, HALF // 2, 2).swapaxes(1, 2).reshape(HALF, HALF)
    density = jnp.concatenate([occupied, virt_density[0, 0]], axis=1)
    own = lax.dynamic_slice_in_dim(integrals, plane * share, share, 0).transpose(1, 0, 2)

    densities = [density] + [across(density, move) for move in range(1, 8)]

    x_zero = across(own[0], 2)
    y_one = across(own[1], 4)
    x_one = across(own[1], 2)
    y_zero = across(own[0], 4)
    d_zero = across(x_zero, 4)
    d_one = across(y_one, 2)
    pieces = {
        0: own,
        2: jnp.stack([x_zero, x_one]),
        4: jnp.stack([y_zero, y_one]),
        6: jnp.stack([d_zero, d_one]),
    }
    for move in (0, 2, 4, 6):
        pieces[move + 1] = across(pieces[move], 1)
    pieces = [pieces[move] for move in range(8)]

    lists = pair_lists.reshape(8, 2, caps)
    mine = lax.dynamic_index_in_dim(lists, device, 0, keepdims=False).T.reshape(-1)
    moves = mine ^ device
    stacked = jnp.stack(densities)
    picked = jnp.zeros((mine.shape[0],) + density.shape, density.dtype)
    for move in range(8):
        picked = jnp.where((moves == move)[:, None, None], stacked[move][None], picked)
    picked = picked.reshape(caps, 2, HALF, LANES)
    per_time = [picked] + [planes(picked, move) for move in range(1, 4)]

    tiles = integrals.transpose(1, 0, 2).reshape(caps, 2, HALF, pair_width)
    tile_spec = pl.BlockSpec((1, 1, HALF, pair_width), lambda a, b: (a, b, 0, 0))
    rows_scratch = pltpu.VMEM((HALF * HALF // 2, LANES), jnp.float32)
    turned = pl.pallas_call(
        turn_kernel,
        grid=(caps, 2),
        out_shape=jax.ShapeDtypeStruct(tiles.shape, tiles.dtype),
        in_specs=[tile_spec],
        out_specs=tile_spec,
        scratch_shapes=[rows_scratch],
        compiler_params=params,
    )(tiles)
    mixed = [
        pl.pallas_call(
            mix_kernel,
            grid=(caps, 2),
            out_shape=jax.ShapeDtypeStruct(tiles.shape, tiles.dtype),
            in_specs=[tile_spec, pl.BlockSpec((1, 1, HALF, LANES), lambda a, b: (a, b, 0, 0))],
            out_specs=tile_spec,
            scratch_shapes=[rows_scratch],
            compiler_params=params,
        )(turned, chosen)
        for chosen in per_time
    ]

    theirs = jnp.stack(
        [
            lax.dynamic_index_in_dim(lists, device ^ move, 0, keepdims=False) for move in range(8)
        ]
    )
    theirs = lax.dynamic_index_in_dim(theirs, plane // 2, 1, keepdims=False)
    match = (mine[:, None, None] == theirs.T[None]).astype(jnp.float32)
    match = jnp.repeat(match.reshape(-1, 8), share, axis=1)
    order = plane ^ jnp.arange(4, dtype=jnp.int32)
    weights = cosine_weights[order][:, order]
    depth = 1024
    columns = 8 * share
    chi = pl.pallas_call(
        gram_kernel,
        grid=(pair_width // depth,),
        out_shape=jax.ShapeDtypeStruct((4, local_count, columns), jnp.bfloat16),
        in_specs=[smem, pl.BlockSpec(match.shape, lambda k: (0, 0))]
        + [pl.BlockSpec((caps, 2, HALF, depth), lambda k: (0, 0, 0, k))] * 4
        + [pl.BlockSpec((caps, share, depth), lambda k: (0, 0, k))] * 8,
        out_specs=pl.BlockSpec((4, local_count, columns), lambda k: (0, 0, 0)),
        scratch_shapes=[pltpu.VMEM((caps, 4, caps * local_count, columns), jnp.float32)],
        compiler_params=params,
    )(weights, match, *mixed, *pieces)

    received = [chi[0]] + [planes(chi[move], move) for move in range(1, 4)]
    grouped = coulomb_blocks.reshape(8, 2, HALF, HALF)
    empty = jnp.zeros((8, HALF, HALF), grouped.dtype)
    factors = jnp.concatenate(
        [
            jnp.concatenate([grouped[:, 0], empty], axis=2),
            jnp.concatenate([empty, grouped[:, 1]], axis=2),
        ],
        axis=1,
    )
    high = factors.astype(jnp.bfloat16)
    low = (factors - high.astype(jnp.float32)).astype(jnp.bfloat16)
    place = jnp.stack([plane, device]).astype(jnp.int32)
    return pl.pallas_call(
        screen_kernel,
        out_shape=jax.ShapeDtypeStruct((1, local_count, 8 * LANES), jnp.float32),
        in_specs=[smem] + [vmem] * 6,
        out_specs=vmem,
        compiler_params=params,
    )(place, *received, high, low)


def per_device(integrals, pair_lists, occ_density, virt_density, cosine_weights, coulomb_blocks):
    planned = (
        lax.axis_size("tm") == 4
        and lax.axis_size("tensor") == 8
        and integrals.shape == (2 * HALF, 2, HALF * HALF)
        and coulomb_blocks.shape == (16, HALF, HALF)
    )
    step = small_slice if planned else any_slice
    return step(integrals, pair_lists, occ_density, virt_density, cosine_weights, coulomb_blocks)


def solution(mesh):
    in_specs = (
        P("tensor", None, None),
        P(),
        P("tm", "tensor", None, None),
        P("tm", "tensor", None, None),
        P(),
        P(),
    )
    out_specs = P("tm", "tensor", None)
    return jax.shard_map(
        per_device, mesh=mesh, in_specs=in_specs, out_specs=out_specs, check_vma=False
    )
```

```python
import functools

import jax
import jax.numpy as jnp
from jax import lax
from jax.experimental import pallas as pl
from jax.experimental.pallas import tpu as pltpu
from jax.sharding import PartitionSpec as P

MOST = 6
HALF = 64
LANES = 128


def listed_blocks(pair_lists, pair_index):
    block_count = pair_lists.shape[0]
    member = jnp.any(pair_lists == pair_index, axis=1)
    positions = jnp.cumsum(member.astype(jnp.int32)) - 1
    slot_ids = jnp.arange(MOST, dtype=jnp.int32)
    matches = member[None, :] & (positions[None, :] == slot_ids[:, None])
    labels = jnp.arange(block_count, dtype=jnp.int32)
    located = jnp.sum(jnp.where(matches, labels[None, :], 0), axis=1)
    return jnp.where(jnp.any(matches, axis=1), located, block_count)


def density_product(row_data, occupied, virtual):
    row_count = row_data.shape[0]
    orbital_width = occupied.shape[0]
    half_done = jnp.dot(
        row_data.reshape(row_count * orbital_width, orbital_width),
        virtual,
        preferred_element_type=jnp.float32,
    )
    half_done = half_done.astype(jnp.bfloat16).reshape(row_count, orbital_width, orbital_width)
    contracted = jnp.einsum("rms,ml->rls", half_done, occupied, preferred_element_type=jnp.float32)
    return contracted.astype(jnp.bfloat16).reshape(row_count, orbital_width * orbital_width)


def pack_rows(local_rows, first_row, pair_lists, pair_count, block_rows):
    row_count = local_rows.shape[0]
    row_ids = first_row + jnp.arange(row_count, dtype=jnp.int32)
    targets = pair_lists[row_ids // block_rows]
    places = jnp.broadcast_to(jnp.arange(row_count, dtype=jnp.int32)[:, None], targets.shape)
    zero_buffer = jnp.zeros((pair_count, row_count, local_rows.shape[2]), local_rows.dtype)
    filled = zero_buffer.at[targets, places].set(local_rows)
    return filled.reshape(pair_count * row_count, local_rows.shape[2])


def any_slice(integrals, pair_lists, occ_density, virt_density, cosine_weights, coulomb_blocks):
    tensor_size = lax.axis_size("tensor")
    owner_pair = lax.axis_index("tensor")
    local_count = integrals.shape[0]
    slab_rows = local_count * tensor_size
    block_count = coulomb_blocks.shape[0]
    block_rows = coulomb_blocks.shape[1]
    occupied = occ_density[0, 0]
    virtual = virt_density[0, 0]
    chosen = listed_blocks(pair_lists, owner_pair)
    wanted = (
        chosen[:, None] * block_rows + jnp.arange(block_rows, dtype=jnp.int32)[None, :]
    ).reshape(-1)
    outgoing = pack_rows(integrals, owner_pair * local_count, pair_lists, tensor_size, block_rows)
    arrived = lax.all_to_all(outgoing, "tensor", split_axis=0, concat_axis=0, tiled=True)
    tile_rows = jnp.take(arrived, wanted, axis=0, mode="fill", fill_value=0)
    weighted = density_product(tile_rows, occupied, virtual)
    gram_block = lax.dot_general(
        weighted, tile_rows, (((1,), (1,)), ((), ())), preferred_element_type=jnp.float32
    )
    most_count = chosen.shape[0]
    block_ids = jnp.arange(block_count, dtype=jnp.int32)
    slot_ids = jnp.arange(most_count, dtype=jnp.int32)
    block_match = chosen[None, :] == block_ids[:, None]
    slot_of = jnp.sum(jnp.where(block_match, slot_ids[None, :], 0), axis=1)
    present = jnp.any(block_match, axis=1)
    slab_ids = jnp.arange(slab_rows, dtype=jnp.int32)
    row_block = slab_ids // block_rows
    source_row = jnp.where(
        present[row_block],
        slot_of[row_block] * block_rows + slab_ids % block_rows,
        most_count * block_rows,
    )
    rounded_terms = gram_block.astype(jnp.bfloat16)
    outgoing_terms = jnp.take(rounded_terms, source_row, axis=0, mode="fill", fill_value=0)
    arrived_terms = lax.all_to_all(
        outgoing_terms, "tensor", split_axis=0, concat_axis=0, tiled=True
    )
    received = arrived_terms.reshape(tensor_size, local_count, most_count, block_rows)
    every_chosen = jax.vmap(lambda pair_index: listed_blocks(pair_lists, pair_index))(
        jnp.arange(tensor_size, dtype=jnp.int32)
    )
    placement = (every_chosen[:, :, None] == block_ids[None, None, :]).astype(jnp.bfloat16)
    placed = jnp.einsum("srja,sjp->rpa", received, placement, preferred_element_type=jnp.float32)
    chi_rows = placed.reshape(local_count, slab_rows)
    spread = jnp.einsum(
        "ft,trc->frc",
        cosine_weights,
        lax.all_to_all(
            chi_rows[None].astype(jnp.bfloat16), "tm", split_axis=2, concat_axis=0, tiled=True
        ).astype(jnp.float32),
        precision=lax.Precision.HIGHEST,
    )
    freq_rows = lax.all_to_all(
        spread.astype(jnp.bfloat16), "tm", split_axis=0, concat_axis=2, tiled=True
    ).astype(spread.dtype)
    shaped = freq_rows.reshape(1, local_count, block_count, block_rows)
    screened = jnp.einsum("frpa,pab->frpb", shaped, coulomb_blocks, precision=lax.Precision.HIGHEST)
    return screened.reshape(1, local_count, slab_rows)


def exchange_halves(even, odd):
    left = lax.broadcasted_iota(jnp.int32, even.shape, 1) < HALF
    first = jnp.where(left, even, pltpu.roll(odd, HALF, 1))
    second = jnp.where(left, pltpu.roll(even, HALF, 1), odd)
    return first, second


def own_kernel(
    rows_ref, occupied_ref, virtual_ref, low_ref, high_ref, density_ref, share_ref, two_ref, done
):
    share = share_ref.shape[0]
    caps, pair_width = share_ref.shape[1:]
    first = pl.multiple_of(lax.axis_index("tm") * share, share)
    copies = [
        pltpu.make_async_copy(rows_ref.at[pl.ds(first, share)], share_ref, done.at[0]),
        pltpu.make_async_copy(occupied_ref.at[0, 0], two_ref.at[0], done.at[1]),
        pltpu.make_async_copy(virtual_ref.at[0, 0], two_ref.at[1], done.at[2]),
    ]
    for copy in copies:
        copy.start()
    for copy in copies[1:]:
        copy.wait()
    both = jnp.concatenate([two_ref[0], two_ref[1]], axis=1)
    density_ref[...] = both
    half = share // 2
    for piece in range(HALF // half):
        place = caps * pair_width + piece * LANES
        block = both[piece * half : (piece + 1) * half]
        low_ref[:, place : place + LANES] = block
        high_ref[:, place : place + LANES] = block
    copies[0].wait()
    width = 1024
    for place in range(0, pair_width, width):
        apart = jnp.swapaxes(share_ref[:, :, place : place + width], 0, 1)
        for column in range(caps):
            lanes = slice(column * pair_width + place, column * pair_width + place + width)
            low_ref[:, lanes] = apart[column, :half]
            high_ref[:, lanes] = apart[column, half:]


def pair_kernel(low_ref, high_ref, x_ref, y_ref, *refs):
    to_x_ref, to_y_ref = refs[-2:]
    caps, pair_width = to_x_ref.shape[1], to_x_ref.shape[3]
    for column in range(caps):
        lanes = slice(column * pair_width, (column + 1) * pair_width)
        to_x_ref[0, column] = high_ref[:, lanes]
        to_x_ref[1, column] = y_ref[:, lanes]
        to_y_ref[0, column] = low_ref[:, lanes]
        to_y_ref[1, column] = x_ref[:, lanes]


def gather_kernel(density_ref, x_ref, y_ref, d_ref, out_ref):
    half = x_ref.shape[0]
    start = x_ref.shape[1] - HALF // half * LANES
    out_ref[0] = density_ref[...]
    out_ref[3] = d_ref[...]
    for piece in range(HALF // half):
        lanes = slice(start + piece * LANES, start + (piece + 1) * LANES)
        out_ref[1, piece * half : (piece + 1) * half] = x_ref[:, lanes]
        out_ref[2, piece * half : (piece + 1) * half] = y_ref[:, lanes]


def order_kernel(x_ref, y_ref, *refs):
    refs[-2][...] = x_ref[...]
    refs[-1][...] = y_ref[...]


def turn_kernel(rows_ref, out_ref, apart_ref):
    caps, parts, count, pair_width = out_ref.shape
    width = 1024
    for place in range(0, pair_width, width):
        block = rows_ref[:, :, place : place + width]
        apart_ref[:, :, place : place + width] = jnp.swapaxes(block, 0, 1)
    for column in range(caps):
        for part in range(parts):
            lanes = [
                apart_ref[column, part * count : (part + 1) * count, place : place + LANES]
                for place in range(0, pair_width, LANES)
            ]
            by_row = jnp.swapaxes(jnp.stack(lanes), 0, 1)
            for low in range(count // 2):
                first, second = exchange_halves(by_row[low], by_row[low + count // 2])
                place = slice(low * LANES, (low + 1) * LANES)
                out_ref[column, part, : count // 2, place] = first
                out_ref[column, part, count // 2 :, place] = second


def pick_kernel(lists_ref, near_ref, core_ref, after_ref, out_ref, all_ref):
    device = lax.axis_index("tensor")
    for move in range(4):
        all_ref[2 * move] = near_ref[move]
        all_ref[2 * move + 1] = core_ref[move]
    row = lax.broadcasted_iota(jnp.int32, (HALF, HALF), 0)
    col = lax.broadcasted_iota(jnp.int32, (HALF, HALF), 1)
    source = 2 * (col % (HALF // 2)) + col // (HALF // 2)
    order = (row == source).astype(jnp.float32).astype(jnp.bfloat16)
    for column in range(out_ref.shape[0]):
        for part in range(out_ref.shape[1]):
            pair = lists_ref[column, 2 * device + part]
            chosen = all_ref[pair ^ device]
            turned = chosen[:, :HALF].astype(jnp.float32).T.astype(jnp.bfloat16)
            moved = jnp.dot(turned, order, preferred_element_type=jnp.float32)
            both = jnp.concatenate([moved, chosen[:, HALF:].astype(jnp.float32)], axis=1)
            out_ref[column, part] = both.astype(jnp.bfloat16)


def mix_kernel(turned_ref, density_ref, out_ref, mark_ref):
    caps, parts, count, pair_width = out_ref.shape
    wide = 4 * HALF
    row_ids = lax.broadcasted_iota(jnp.int32, (wide, wide), 0) // HALF
    col_ids = lax.broadcasted_iota(jnp.int32, (wide, wide), 1) // HALF
    groups = pair_width // wide
    mark_ref[...] = jnp.zeros_like(mark_ref)
    for column in range(caps):
        for part in range(parts):
            occupied = density_ref[column, part, :, :HALF]
            virtual = density_ref[column, part, :, HALF:].astype(jnp.float32)
            twice = jnp.concatenate([virtual, virtual], axis=1)
            strip = jnp.concatenate([twice, twice], axis=1)
            tiled = jnp.concatenate([strip, strip, strip, strip], axis=0)
            diagonal = jnp.where(row_ids == col_ids, tiled, 0.0).astype(jnp.bfloat16)
            halves = []
            for group in range(groups):
                half_done = jnp.dot(
                    occupied,
                    turned_ref[column, part, :, group * wide : (group + 1) * wide],
                    preferred_element_type=jnp.float32,
                )
                halves.append(half_done.astype(jnp.bfloat16))
            mixed = jnp.dot(
                jnp.concatenate(halves, axis=0), diagonal, preferred_element_type=jnp.float32
            ).astype(jnp.bfloat16)
            near = mixed[:, :LANES].reshape(groups, HALF, LANES)
            far = mixed[:, LANES:].reshape(groups, HALF, LANES)
            by_row = jnp.stack([near, far], axis=1).reshape(2 * groups, HALF, LANES)
            by_row = jnp.swapaxes(by_row, 0, 1)
            for pair in range(HALF // 2):
                first, second = exchange_halves(by_row[2 * pair], by_row[2 * pair + 1])
                place = slice(pair * LANES, (pair + 1) * LANES)
                out_ref[column, part, : count // 2, place] = first
                out_ref[column, part, count // 2 :, place] = second


def gram_kernel(weights_ref, lists_ref, *refs):
    mixed_refs, near_refs, core_refs, out_ref = refs[:4], refs[4:8], refs[8:12], refs[12]
    plane = lax.axis_index("tm")
    device = lax.axis_index("tensor")
    caps = mixed_refs[0].shape[0]
    rows, columns = out_ref.shape[1:]
    owner = lax.broadcasted_iota(jnp.int32, (1, columns), 1) // (columns // 8)
    for part in range(rows // HALF):
        chi = [None] * 4
        for mine in range(caps):
            pair = lists_ref[mine, 2 * device + part]
            listed = jnp.zeros((1, columns), jnp.int32)
            right = []
            for move in range(8):
                block = 2 * (device ^ move) + plane // 2
                second = (lists_ref[1, block] == pair).astype(jnp.int32)
                either = second + (lists_ref[0, block] == pair).astype(jnp.int32)
                listed = jnp.where(owner == move, either, listed)
                to_x, to_y, from_x, from_y = core_refs if move % 2 else near_refs
                halves = (
                    (to_y.at[0], to_x.at[0]),
                    (to_y.at[1], from_x.at[0]),
                    (from_y.at[0], to_x.at[1]),
                    (from_y.at[1], from_x.at[1]),
                )[move // 2]
                right += [half[second] for half in halves]
            left = [mixed[mine, part] for mixed in mixed_refs]
            found = lax.dot_general(
                jnp.concatenate(left, axis=0),
                jnp.concatenate(right, axis=0),
                (((1,), (1,)), ((), ())),
                preferred_element_type=jnp.float32,
            )
            found = jnp.where(listed > 0, found, 0.0)
            for time in range(4):
                term = found[time * HALF : (time + 1) * HALF]
                chi[time] = term if chi[time] is None else chi[time] + term
        for freq in range(4):
            value = weights_ref[plane ^ freq, plane] * chi[0]
            for time in range(1, 4):
                value = value + weights_ref[plane ^ freq, plane ^ time] * chi[time]
            out_ref[freq, part * HALF : (part + 1) * HALF, :] = value.astype(out_ref.dtype)


def screen_kernel(chi_ref, r1, r2, r3, factor_ref, out_ref):
    plane = lax.axis_index("tm")
    device = lax.axis_index("tensor")
    share = r1.shape[1] // 8
    for move in range(8):
        owner = device ^ move
        sums = []
        for pair in ((0, 1), (2, 3)):
            total = None
            for slot in pair:
                other = plane ^ slot
                source = chi_ref.at[0] if slot == 0 else (r1, r2, r3)[slot - 1]
                left = source[:, move * share : (move + 1) * share]
                first = pl.multiple_of((other % 2) * share, share)
                factor = factor_ref[2 * owner + other // 2, pl.ds(first, share), :]
                term = jnp.dot(
                    left, factor.astype(jnp.bfloat16), preferred_element_type=jnp.float32
                )
                total = term if total is None else total + term
            sums.append(total)
        low = jnp.where(plane < 2, sums[0], sums[1])
        high = jnp.where(plane < 2, sums[1], sums[0])
        place = pl.ds(pl.multiple_of(owner * LANES, LANES), LANES)
        out_ref[0, :, place] = jnp.concatenate([low, high], axis=1)


def small_slice(integrals, pair_lists, occ_density, virt_density, cosine_weights, coulomb_blocks):
    local_count, caps, pair_width = integrals.shape
    share = local_count // 4
    columns = 8 * share
    vmem = pl.BlockSpec(memory_space=pltpu.VMEM)
    smem = pl.BlockSpec(memory_space=pltpu.SMEM)
    tiles = jax.ShapeDtypeStruct((caps, 2, HALF, pair_width), jnp.bfloat16)

    def kernel(body, out_shape, in_specs, microseconds, scratch=(), room=16):
        return pl.pallas_call(
            body,
            out_shape=out_shape,
            in_specs=in_specs,
            out_specs=jax.tree.map(lambda _: vmem, out_shape),
            scratch_shapes=list(scratch),
            compiler_params=pltpu.CompilerParams(vmem_limit_bytes=room * 1024 * 1024),
            cost_estimate=pl.CostEstimate(
                flops=int(microseconds * 1e9), bytes_accessed=0, transcendentals=0
            ),
        )

    def across(array, move):
        return lax.ppermute(array, "tensor", [(i, i ^ move) for i in range(8)])

    def planes(array, move):
        return lax.ppermute(array, "tm", [(i, i ^ move) for i in range(4)])

    lists = pair_lists.T
    half = share // 2
    message = jax.ShapeDtypeStruct(
        (half, caps * pair_width + HALF // half * LANES), jnp.bfloat16
    )
    block = jax.ShapeDtypeStruct((HALF, LANES), jnp.bfloat16)
    both = jax.ShapeDtypeStruct((2, caps, half, pair_width), jnp.bfloat16)
    low, high, density = kernel(
        own_kernel,
        [message, message, block],
        [pl.BlockSpec(memory_space=pltpu.HBM)] * 3,
        2,
        [
            pltpu.VMEM((share, caps, pair_width), jnp.bfloat16),
            pltpu.VMEM((2, HALF, HALF), jnp.bfloat16),
            pltpu.SemaphoreType.DMA((3,)),
        ],
        room=62,
    )(integrals, occ_density, virt_density)
    x_low = across(low, 2)
    y_high = across(high, 4)
    turned = kernel(
        turn_kernel, tiles, [vmem], 1.2, [pltpu.VMEM((caps, local_count, pair_width), jnp.bfloat16)]
    )(integrals)
    near = kernel(
        gather_kernel, jax.ShapeDtypeStruct((4, HALF, LANES), jnp.bfloat16), [vmem] * 4, 0.2
    )(density, x_low, y_high, across(density, 6))
    to_x, to_y = kernel(pair_kernel, [both] * 2, [vmem] * 6, 0.3)(
        low, high, x_low, y_high, turned, near
    )
    picked = kernel(
        pick_kernel,
        jax.ShapeDtypeStruct((caps, 2, HALF, LANES), jnp.bfloat16),
        [smem] + [vmem] * 3,
        1,
        [pltpu.VMEM((8, HALF, LANES), jnp.bfloat16)],
    )(lists, near, across(near, 1), to_x)
    per_time = [picked] + [planes(picked, move) for move in range(1, 4)]

    mark = jax.ShapeDtypeStruct((8, LANES), jnp.float32)
    mixed, marks = zip(
        *[kernel(mix_kernel, [tiles, mark], [vmem] * 2, 0.1)(turned, each) for each in per_time]
    )

    from_x, from_y = kernel(order_kernel, [both] * 2, [vmem] * 6, 0.3)(
        across(to_x, 2), across(to_y, 4), *marks[:3], per_time[3]
    )
    pieces = [to_x, to_y, from_x, from_y]
    chi = kernel(
        gram_kernel,
        jax.ShapeDtypeStruct((4, local_count, columns), jnp.bfloat16),
        [smem, smem] + [vmem] * 12,
        3,
    )(cosine_weights, lists, *mixed, *pieces, *[across(piece, 1) for piece in pieces])

    received = [planes(chi[move], move) for move in range(1, 4)]
    return kernel(
        screen_kernel,
        jax.ShapeDtypeStruct((1, local_count, 8 * LANES), jnp.float32),
        [vmem] * 5,
        1,
    )(chi, *received, coulomb_blocks)


def per_device(integrals, pair_lists, occ_density, virt_density, cosine_weights, coulomb_blocks):
    planned = (
        lax.axis_size("tm") == 4
        and lax.axis_size("tensor") == 8
        and integrals.shape == (2 * HALF, 2, HALF * HALF)
        and coulomb_blocks.shape == (16, HALF, HALF)
    )
    step = small_slice if planned else any_slice
    return step(integrals, pair_lists, occ_density, virt_density, cosine_weights, coulomb_blocks)


def solution(mesh):
    in_specs = (
        P("tensor", None, None),
        P(),
        P("tm", "tensor", None, None),
        P("tm", "tensor", None, None),
        P(),
        P(),
    )
    out_specs = P("tm", "tensor", None)
    return jax.shard_map(
        per_device, mesh=mesh, in_specs=in_specs, out_specs=out_specs, check_vma=False
    )
```

```python
import functools

import jax
import jax.numpy as jnp
from jax import lax
from jax.experimental import pallas as pl
from jax.experimental.pallas import tpu as pltpu
from jax.sharding import PartitionSpec as P

MOST = 6
HALF = 64
LANES = 128


def listed_blocks(pair_lists, pair_index):
    block_count = pair_lists.shape[0]
    member = jnp.any(pair_lists == pair_index, axis=1)
    positions = jnp.cumsum(member.astype(jnp.int32)) - 1
    slot_ids = jnp.arange(MOST, dtype=jnp.int32)
    matches = member[None, :] & (positions[None, :] == slot_ids[:, None])
    labels = jnp.arange(block_count, dtype=jnp.int32)
    located = jnp.sum(jnp.where(matches, labels[None, :], 0), axis=1)
    return jnp.where(jnp.any(matches, axis=1), located, block_count)


def density_product(row_data, occupied, virtual):
    row_count = row_data.shape[0]
    orbital_width = occupied.shape[0]
    half_done = jnp.dot(
        row_data.reshape(row_count * orbital_width, orbital_width),
        virtual,
        preferred_element_type=jnp.float32,
    )
    half_done = half_done.astype(jnp.bfloat16).reshape(row_count, orbital_width, orbital_width)
    contracted = jnp.einsum("rms,ml->rls", half_done, occupied, preferred_element_type=jnp.float32)
    return contracted.astype(jnp.bfloat16).reshape(row_count, orbital_width * orbital_width)


def pack_rows(local_rows, first_row, pair_lists, pair_count, block_rows):
    row_count = local_rows.shape[0]
    row_ids = first_row + jnp.arange(row_count, dtype=jnp.int32)
    targets = pair_lists[row_ids // block_rows]
    places = jnp.broadcast_to(jnp.arange(row_count, dtype=jnp.int32)[:, None], targets.shape)
    zero_buffer = jnp.zeros((pair_count, row_count, local_rows.shape[2]), local_rows.dtype)
    filled = zero_buffer.at[targets, places].set(local_rows)
    return filled.reshape(pair_count * row_count, local_rows.shape[2])


def any_slice(integrals, pair_lists, occ_density, virt_density, cosine_weights, coulomb_blocks):
    tensor_size = lax.axis_size("tensor")
    owner_pair = lax.axis_index("tensor")
    local_count = integrals.shape[0]
    slab_rows = local_count * tensor_size
    block_count = coulomb_blocks.shape[0]
    block_rows = coulomb_blocks.shape[1]
    occupied = occ_density[0, 0]
    virtual = virt_density[0, 0]
    chosen = listed_blocks(pair_lists, owner_pair)
    wanted = (
        chosen[:, None] * block_rows + jnp.arange(block_rows, dtype=jnp.int32)[None, :]
    ).reshape(-1)
    outgoing = pack_rows(integrals, owner_pair * local_count, pair_lists, tensor_size, block_rows)
    arrived = lax.all_to_all(outgoing, "tensor", split_axis=0, concat_axis=0, tiled=True)
    tile_rows = jnp.take(arrived, wanted, axis=0, mode="fill", fill_value=0)
    weighted = density_product(tile_rows, occupied, virtual)
    gram_block = lax.dot_general(
        weighted, tile_rows, (((1,), (1,)), ((), ())), preferred_element_type=jnp.float32
    )
    most_count = chosen.shape[0]
    block_ids = jnp.arange(block_count, dtype=jnp.int32)
    slot_ids = jnp.arange(most_count, dtype=jnp.int32)
    block_match = chosen[None, :] == block_ids[:, None]
    slot_of = jnp.sum(jnp.where(block_match, slot_ids[None, :], 0), axis=1)
    present = jnp.any(block_match, axis=1)
    slab_ids = jnp.arange(slab_rows, dtype=jnp.int32)
    row_block = slab_ids // block_rows
    source_row = jnp.where(
        present[row_block],
        slot_of[row_block] * block_rows + slab_ids % block_rows,
        most_count * block_rows,
    )
    rounded_terms = gram_block.astype(jnp.bfloat16)
    outgoing_terms = jnp.take(rounded_terms, source_row, axis=0, mode="fill", fill_value=0)
    arrived_terms = lax.all_to_all(
        outgoing_terms, "tensor", split_axis=0, concat_axis=0, tiled=True
    )
    received = arrived_terms.reshape(tensor_size, local_count, most_count, block_rows)
    every_chosen = jax.vmap(lambda pair_index: listed_blocks(pair_lists, pair_index))(
        jnp.arange(tensor_size, dtype=jnp.int32)
    )
    placement = (every_chosen[:, :, None] == block_ids[None, None, :]).astype(jnp.bfloat16)
    placed = jnp.einsum("srja,sjp->rpa", received, placement, preferred_element_type=jnp.float32)
    chi_rows = placed.reshape(local_count, slab_rows)
    spread = jnp.einsum(
        "ft,trc->frc",
        cosine_weights,
        lax.all_to_all(
            chi_rows[None].astype(jnp.bfloat16), "tm", split_axis=2, concat_axis=0, tiled=True
        ).astype(jnp.float32),
        precision=lax.Precision.HIGHEST,
    )
    freq_rows = lax.all_to_all(
        spread.astype(jnp.bfloat16), "tm", split_axis=0, concat_axis=2, tiled=True
    ).astype(spread.dtype)
    shaped = freq_rows.reshape(1, local_count, block_count, block_rows)
    screened = jnp.einsum("frpa,pab->frpb", shaped, coulomb_blocks, precision=lax.Precision.HIGHEST)
    return screened.reshape(1, local_count, slab_rows)


def exchange_halves(even, odd):
    left = lax.broadcasted_iota(jnp.int32, even.shape, 1) < HALF
    first = jnp.where(left, even, pltpu.roll(odd, HALF, 1))
    second = jnp.where(left, pltpu.roll(even, HALF, 1), odd)
    return first, second


def own_kernel(
    rows_ref, occupied_ref, virtual_ref, low_ref, high_ref, density_ref, share_ref, two_ref, done
):
    share = share_ref.shape[0]
    caps, pair_width = share_ref.shape[1:]
    first = pl.multiple_of(lax.axis_index("tm") * share, share)
    copies = [
        pltpu.make_async_copy(rows_ref.at[pl.ds(first, share)], share_ref, done.at[0]),
        pltpu.make_async_copy(occupied_ref.at[0, 0], two_ref.at[0], done.at[1]),
        pltpu.make_async_copy(virtual_ref.at[0, 0], two_ref.at[1], done.at[2]),
    ]
    for copy in copies:
        copy.start()
    for copy in copies[1:]:
        copy.wait()
    row = lax.broadcasted_iota(jnp.int32, (HALF, HALF), 0)
    col = lax.broadcasted_iota(jnp.int32, (HALF, HALF), 1)
    source = 2 * (col % (HALF // 2)) + col // (HALF // 2)
    order = (row == source).astype(jnp.float32).astype(jnp.bfloat16)
    turned = two_ref[0].astype(jnp.float32).T.astype(jnp.bfloat16)
    moved = jnp.dot(turned, order, preferred_element_type=jnp.float32)
    both = jnp.concatenate([moved, two_ref[1].astype(jnp.float32)], axis=1).astype(jnp.bfloat16)
    density_ref[...] = both
    half = share // 2
    for piece in range(HALF // half):
        place = caps * pair_width + piece * LANES
        block = both[piece * half : (piece + 1) * half]
        low_ref[:, place : place + LANES] = block
        high_ref[:, place : place + LANES] = block
    copies[0].wait()
    width = 1024
    for place in range(0, pair_width, width):
        apart = jnp.swapaxes(share_ref[:, :, place : place + width], 0, 1)
        for column in range(caps):
            lanes = slice(column * pair_width + place, column * pair_width + place + width)
            low_ref[:, lanes] = apart[column, :half]
            high_ref[:, lanes] = apart[column, half:]


def pair_kernel(low_ref, high_ref, x_ref, y_ref, *refs):
    to_x_ref, to_y_ref = refs[-2:]
    caps, pair_width = to_x_ref.shape[1], to_x_ref.shape[3]
    for column in range(caps):
        lanes = slice(column * pair_width, (column + 1) * pair_width)
        to_x_ref[0, column] = high_ref[:, lanes]
        to_x_ref[1, column] = y_ref[:, lanes]
        to_y_ref[0, column] = low_ref[:, lanes]
        to_y_ref[1, column] = x_ref[:, lanes]


def gather_kernel(density_ref, x_ref, y_ref, d_ref, out_ref):
    half = x_ref.shape[0]
    start = x_ref.shape[1] - HALF // half * LANES
    out_ref[0] = density_ref[...]
    out_ref[3] = d_ref[...]
    for piece in range(HALF // half):
        lanes = slice(start + piece * LANES, start + (piece + 1) * LANES)
        out_ref[1, piece * half : (piece + 1) * half] = x_ref[:, lanes]
        out_ref[2, piece * half : (piece + 1) * half] = y_ref[:, lanes]


def order_kernel(x_ref, y_ref, *refs):
    refs[-2][...] = x_ref[...]
    refs[-1][...] = y_ref[...]


def turn_kernel(rows_ref, out_ref, apart_ref):
    caps, parts, count, pair_width = out_ref.shape
    width = 1024
    for place in range(0, pair_width, width):
        block = rows_ref[:, :, place : place + width]
        apart_ref[:, :, place : place + width] = jnp.swapaxes(block, 0, 1)
    for column in range(caps):
        for part in range(parts):
            lanes = [
                apart_ref[column, part * count : (part + 1) * count, place : place + LANES]
                for place in range(0, pair_width, LANES)
            ]
            by_row = jnp.swapaxes(jnp.stack(lanes), 0, 1)
            for low in range(count // 2):
                first, second = exchange_halves(by_row[low], by_row[low + count // 2])
                place = slice(low * LANES, (low + 1) * LANES)
                out_ref[column, part, : count // 2, place] = first
                out_ref[column, part, count // 2 :, place] = second


def pick_kernel(lists_ref, near_ref, core_ref, after_ref, out_ref, all_ref):
    device = lax.axis_index("tensor")
    for move in range(4):
        all_ref[2 * move] = near_ref[move]
        all_ref[2 * move + 1] = core_ref[move]
    for column in range(out_ref.shape[0]):
        for part in range(out_ref.shape[1]):
            pair = lists_ref[column, 2 * device + part]
            out_ref[column, part] = all_ref[pair ^ device]


def mix_kernel(turned_ref, density_ref, out_ref, mark_ref):
    caps, parts, count, pair_width = out_ref.shape
    wide = 4 * HALF
    row_ids = lax.broadcasted_iota(jnp.int32, (wide, wide), 0) // HALF
    col_ids = lax.broadcasted_iota(jnp.int32, (wide, wide), 1) // HALF
    groups = pair_width // wide
    mark_ref[...] = jnp.zeros_like(mark_ref)
    for column in range(caps):
        for part in range(parts):
            occupied = density_ref[column, part, :, :HALF]
            virtual = density_ref[column, part, :, HALF:].astype(jnp.float32)
            twice = jnp.concatenate([virtual, virtual], axis=1)
            strip = jnp.concatenate([twice, twice], axis=1)
            tiled = jnp.concatenate([strip, strip, strip, strip], axis=0)
            diagonal = jnp.where(row_ids == col_ids, tiled, 0.0).astype(jnp.bfloat16)
            halves = []
            for group in range(groups):
                half_done = jnp.dot(
                    occupied,
                    turned_ref[column, part, :, group * wide : (group + 1) * wide],
                    preferred_element_type=jnp.float32,
                )
                halves.append(half_done.astype(jnp.bfloat16))
            mixed = jnp.dot(
                jnp.concatenate(halves, axis=0), diagonal, preferred_element_type=jnp.float32
            ).astype(jnp.bfloat16)
            near = mixed[:, :LANES].reshape(groups, HALF, LANES)
            far = mixed[:, LANES:].reshape(groups, HALF, LANES)
            by_row = jnp.stack([near, far], axis=1).reshape(2 * groups, HALF, LANES)
            by_row = jnp.swapaxes(by_row, 0, 1)
            for pair in range(HALF // 2):
                first, second = exchange_halves(by_row[2 * pair], by_row[2 * pair + 1])
                place = slice(pair * LANES, (pair + 1) * LANES)
                out_ref[column, part, : count // 2, place] = first
                out_ref[column, part, count // 2 :, place] = second


def gram_kernel(weights_ref, lists_ref, *refs):
    mixed_refs, near_refs, core_refs, out_ref = refs[:4], refs[4:8], refs[8:12], refs[12]
    plane = lax.axis_index("tm")
    device = lax.axis_index("tensor")
    caps = mixed_refs[0].shape[0]
    rows, columns = out_ref.shape[1:]
    owner = lax.broadcasted_iota(jnp.int32, (1, columns), 1) // (columns // 8)
    for part in range(rows // HALF):
        chi = [None] * 4
        for mine in range(caps):
            pair = lists_ref[mine, 2 * device + part]
            listed = jnp.zeros((1, columns), jnp.int32)
            right = []
            for move in range(8):
                block = 2 * (device ^ move) + plane // 2
                second = (lists_ref[1, block] == pair).astype(jnp.int32)
                either = second + (lists_ref[0, block] == pair).astype(jnp.int32)
                listed = jnp.where(owner == move, either, listed)
                to_x, to_y, from_x, from_y = core_refs if move % 2 else near_refs
                halves = (
                    (to_y.at[0], to_x.at[0]),
                    (to_y.at[1], from_x.at[0]),
                    (from_y.at[0], to_x.at[1]),
                    (from_y.at[1], from_x.at[1]),
                )[move // 2]
                right += [half[second] for half in halves]
            left = [mixed[mine, part] for mixed in mixed_refs]
            found = lax.dot_general(
                jnp.concatenate(left, axis=0),
                jnp.concatenate(right, axis=0),
                (((1,), (1,)), ((), ())),
                preferred_element_type=jnp.float32,
            )
            found = jnp.where(listed > 0, found, 0.0)
            for time in range(4):
                term = found[time * HALF : (time + 1) * HALF]
                chi[time] = term if chi[time] is None else chi[time] + term
        for freq in range(4):
            value = weights_ref[plane ^ freq, plane] * chi[0]
            for time in range(1, 4):
                value = value + weights_ref[plane ^ freq, plane ^ time] * chi[time]
            out_ref[freq, part * HALF : (part + 1) * HALF, :] = value.astype(out_ref.dtype)


def factor_kernel(factor_ref, out_ref):
    plane = lax.axis_index("tm")
    device = lax.axis_index("tensor")
    share = out_ref.shape[1] // 8
    out_ref[...] = jnp.zeros_like(out_ref)
    right = lax.broadcasted_iota(jnp.int32, (share, LANES), 1) // HALF
    for slot in range(4):
        other = plane ^ slot
        first = pl.multiple_of((other % 2) * share, share)
        for move in range(8):
            factor = factor_ref[2 * (device ^ move) + other // 2, pl.ds(first, share), :]
            wide = jnp.where(right == other // 2, jnp.concatenate([factor, factor], axis=1), 0.0)
            rows = slice(move * share, (move + 1) * share)
            out_ref[slot, rows, move * LANES : (move + 1) * LANES] = wide.astype(out_ref.dtype)


def screen_kernel(chi_ref, r1, r2, r3, factor_ref, out_ref, block_ref, done):
    device = lax.axis_index("tensor")
    sources = [chi_ref[0], r1[...], r2[...], r3[...]]
    copies = []
    for pair in range(4):
        lanes = slice(2 * pair * LANES, 2 * (pair + 1) * LANES)
        total = None
        for slot in range(4):
            term = jnp.dot(
                sources[slot], factor_ref[slot, :, lanes], preferred_element_type=jnp.float32
            )
            total = term if total is None else total + term
        for side in range(2):
            move = 2 * pair + side
            block_ref[move] = total[:, side * LANES : (side + 1) * LANES]
            place = pl.ds(pl.multiple_of((device ^ move) * LANES, LANES), LANES)
            copies.append(
                pltpu.make_async_copy(block_ref.at[move], out_ref.at[0, :, place], done.at[move])
            )
            copies[-1].start()
    for copy in copies:
        copy.wait()


def small_slice(integrals, pair_lists, occ_density, virt_density, cosine_weights, coulomb_blocks):
    local_count, caps, pair_width = integrals.shape
    share = local_count // 4
    columns = 8 * share
    vmem = pl.BlockSpec(memory_space=pltpu.VMEM)
    smem = pl.BlockSpec(memory_space=pltpu.SMEM)
    tiles = jax.ShapeDtypeStruct((caps, 2, HALF, pair_width), jnp.bfloat16)

    def kernel(body, out_shape, in_specs, microseconds, scratch=(), room=16, **options):
        options = {"out_specs": jax.tree.map(lambda _: vmem, out_shape), **options}
        return pl.pallas_call(
            body,
            out_shape=out_shape,
            in_specs=in_specs,
            scratch_shapes=list(scratch),
            compiler_params=pltpu.CompilerParams(vmem_limit_bytes=room * 1024 * 1024),
            cost_estimate=pl.CostEstimate(
                flops=int(microseconds * 1e9), bytes_accessed=0, transcendentals=0
            ),
            **options,
        )

    def across(array, move):
        return lax.ppermute(array, "tensor", [(i, i ^ move) for i in range(8)])

    def planes(array, move):
        return lax.ppermute(array, "tm", [(i, i ^ move) for i in range(4)])

    lists = pair_lists.T
    half = share // 2
    message = jax.ShapeDtypeStruct(
        (half, caps * pair_width + HALF // half * LANES), jnp.bfloat16
    )
    block = jax.ShapeDtypeStruct((HALF, LANES), jnp.bfloat16)
    both = jax.ShapeDtypeStruct((2, caps, half, pair_width), jnp.bfloat16)
    low, high, density = kernel(
        own_kernel,
        [message, message, block],
        [pl.BlockSpec(memory_space=pltpu.HBM)] * 3,
        2,
        [
            pltpu.VMEM((share, caps, pair_width), jnp.bfloat16),
            pltpu.VMEM((2, HALF, HALF), jnp.bfloat16),
            pltpu.SemaphoreType.DMA((3,)),
        ],
        room=61,
    )(integrals, occ_density, virt_density)
    x_low = across(low, 2)
    y_high = across(high, 4)
    turned = kernel(
        turn_kernel, tiles, [vmem], 1.2, [pltpu.VMEM((caps, local_count, pair_width), jnp.bfloat16)]
    )(integrals)
    near = kernel(
        gather_kernel, jax.ShapeDtypeStruct((4, HALF, LANES), jnp.bfloat16), [vmem] * 4, 0.2
    )(density, x_low, y_high, across(density, 6))
    factors = kernel(
        factor_kernel, jax.ShapeDtypeStruct((4, columns, 8 * LANES), jnp.bfloat16), [vmem], 1
    )(coulomb_blocks)
    to_x, to_y = kernel(pair_kernel, [both] * 2, [vmem] * 7, 0.3)(
        low, high, x_low, y_high, turned, near, factors
    )
    picked = kernel(
        pick_kernel,
        jax.ShapeDtypeStruct((caps, 2, HALF, LANES), jnp.bfloat16),
        [smem] + [vmem] * 3,
        1,
        [pltpu.VMEM((8, HALF, LANES), jnp.bfloat16)],
    )(lists, near, across(near, 1), to_x)
    per_time = [picked] + [planes(picked, move) for move in range(1, 4)]

    mark = jax.ShapeDtypeStruct((8, LANES), jnp.float32)
    mixed, marks = zip(
        *[kernel(mix_kernel, [tiles, mark], [vmem] * 2, 0.1)(turned, each) for each in per_time]
    )

    from_x, from_y = kernel(order_kernel, [both] * 2, [vmem] * 6, 0.3)(
        across(to_x, 2), across(to_y, 4), *marks[:3], per_time[3]
    )
    pieces = [to_x, to_y, from_x, from_y]
    chi = kernel(
        gram_kernel,
        jax.ShapeDtypeStruct((4, local_count, columns), jnp.bfloat16),
        [smem, smem] + [vmem] * 12,
        3,
    )(cosine_weights, lists, *mixed, *pieces, *[across(piece, 1) for piece in pieces])

    received = [planes(chi[move], move) for move in range(1, 4)]
    return kernel(
        screen_kernel,
        jax.ShapeDtypeStruct((1, local_count, 8 * LANES), jnp.float32),
        [vmem] * 5,
        1,
        [pltpu.VMEM((8, local_count, LANES), jnp.float32), pltpu.SemaphoreType.DMA((8,))],
        out_specs=pl.BlockSpec(memory_space=pltpu.HBM),
    )(chi, *received, factors)


def per_device(integrals, pair_lists, occ_density, virt_density, cosine_weights, coulomb_blocks):
    planned = (
        lax.axis_size("tm") == 4
        and lax.axis_size("tensor") == 8
        and integrals.shape == (2 * HALF, 2, HALF * HALF)
        and coulomb_blocks.shape == (16, HALF, HALF)
    )
    step = small_slice if planned else any_slice
    return step(integrals, pair_lists, occ_density, virt_density, cosine_weights, coulomb_blocks)


def solution(mesh):
    in_specs = (
        P("tensor", None, None),
        P(),
        P("tm", "tensor", None, None),
        P("tm", "tensor", None, None),
        P(),
        P(),
    )
    out_specs = P("tm", "tensor", None)
    return jax.shard_map(
        per_device, mesh=mesh, in_specs=in_specs, out_specs=out_specs, check_vma=False
    )
```

```python
import functools

import jax
import jax.numpy as jnp
from jax import lax
from jax.experimental import pallas as pl
from jax.experimental.pallas import tpu as pltpu
from jax.sharding import PartitionSpec as P

MOST = 6
HALF = 64
LANES = 128


def listed_blocks(pair_lists, pair_index):
    block_count = pair_lists.shape[0]
    member = jnp.any(pair_lists == pair_index, axis=1)
    positions = jnp.cumsum(member.astype(jnp.int32)) - 1
    slot_ids = jnp.arange(MOST, dtype=jnp.int32)
    matches = member[None, :] & (positions[None, :] == slot_ids[:, None])
    labels = jnp.arange(block_count, dtype=jnp.int32)
    located = jnp.sum(jnp.where(matches, labels[None, :], 0), axis=1)
    return jnp.where(jnp.any(matches, axis=1), located, block_count)


def density_product(row_data, occupied, virtual):
    row_count = row_data.shape[0]
    orbital_width = occupied.shape[0]
    half_done = jnp.dot(
        row_data.reshape(row_count * orbital_width, orbital_width),
        virtual,
        preferred_element_type=jnp.float32,
    )
    half_done = half_done.astype(jnp.bfloat16).reshape(row_count, orbital_width, orbital_width)
    contracted = jnp.einsum("rms,ml->rls", half_done, occupied, preferred_element_type=jnp.float32)
    return contracted.astype(jnp.bfloat16).reshape(row_count, orbital_width * orbital_width)


def pack_rows(local_rows, first_row, pair_lists, pair_count, block_rows):
    row_count = local_rows.shape[0]
    row_ids = first_row + jnp.arange(row_count, dtype=jnp.int32)
    targets = pair_lists[row_ids // block_rows]
    places = jnp.broadcast_to(jnp.arange(row_count, dtype=jnp.int32)[:, None], targets.shape)
    zero_buffer = jnp.zeros((pair_count, row_count, local_rows.shape[2]), local_rows.dtype)
    filled = zero_buffer.at[targets, places].set(local_rows)
    return filled.reshape(pair_count * row_count, local_rows.shape[2])


def any_slice(integrals, pair_lists, occ_density, virt_density, cosine_weights, coulomb_blocks):
    tensor_size = lax.axis_size("tensor")
    owner_pair = lax.axis_index("tensor")
    local_count = integrals.shape[0]
    slab_rows = local_count * tensor_size
    block_count = coulomb_blocks.shape[0]
    block_rows = coulomb_blocks.shape[1]
    occupied = occ_density[0, 0]
    virtual = virt_density[0, 0]
    chosen = listed_blocks(pair_lists, owner_pair)
    wanted = (
        chosen[:, None] * block_rows + jnp.arange(block_rows, dtype=jnp.int32)[None, :]
    ).reshape(-1)
    outgoing = pack_rows(integrals, owner_pair * local_count, pair_lists, tensor_size, block_rows)
    arrived = lax.all_to_all(outgoing, "tensor", split_axis=0, concat_axis=0, tiled=True)
    tile_rows = jnp.take(arrived, wanted, axis=0, mode="fill", fill_value=0)
    weighted = density_product(tile_rows, occupied, virtual)
    gram_block = lax.dot_general(
        weighted, tile_rows, (((1,), (1,)), ((), ())), preferred_element_type=jnp.float32
    )
    most_count = chosen.shape[0]
    block_ids = jnp.arange(block_count, dtype=jnp.int32)
    slot_ids = jnp.arange(most_count, dtype=jnp.int32)
    block_match = chosen[None, :] == block_ids[:, None]
    slot_of = jnp.sum(jnp.where(block_match, slot_ids[None, :], 0), axis=1)
    present = jnp.any(block_match, axis=1)
    slab_ids = jnp.arange(slab_rows, dtype=jnp.int32)
    row_block = slab_ids // block_rows
    source_row = jnp.where(
        present[row_block],
        slot_of[row_block] * block_rows + slab_ids % block_rows,
        most_count * block_rows,
    )
    rounded_terms = gram_block.astype(jnp.bfloat16)
    outgoing_terms = jnp.take(rounded_terms, source_row, axis=0, mode="fill", fill_value=0)
    arrived_terms = lax.all_to_all(
        outgoing_terms, "tensor", split_axis=0, concat_axis=0, tiled=True
    )
    received = arrived_terms.reshape(tensor_size, local_count, most_count, block_rows)
    every_chosen = jax.vmap(lambda pair_index: listed_blocks(pair_lists, pair_index))(
        jnp.arange(tensor_size, dtype=jnp.int32)
    )
    placement = (every_chosen[:, :, None] == block_ids[None, None, :]).astype(jnp.bfloat16)
    placed = jnp.einsum("srja,sjp->rpa", received, placement, preferred_element_type=jnp.float32)
    chi_rows = placed.reshape(local_count, slab_rows)
    spread = jnp.einsum(
        "ft,trc->frc",
        cosine_weights,
        lax.all_to_all(
            chi_rows[None].astype(jnp.bfloat16), "tm", split_axis=2, concat_axis=0, tiled=True
        ).astype(jnp.float32),
        precision=lax.Precision.HIGHEST,
    )
    freq_rows = lax.all_to_all(
        spread.astype(jnp.bfloat16), "tm", split_axis=0, concat_axis=2, tiled=True
    ).astype(spread.dtype)
    shaped = freq_rows.reshape(1, local_count, block_count, block_rows)
    screened = jnp.einsum("frpa,pab->frpb", shaped, coulomb_blocks, precision=lax.Precision.HIGHEST)
    return screened.reshape(1, local_count, slab_rows)


def exchange_halves(even, odd):
    left = lax.broadcasted_iota(jnp.int32, even.shape, 1) < HALF
    first = jnp.where(left, even, pltpu.roll(odd, HALF, 1))
    second = jnp.where(left, pltpu.roll(even, HALF, 1), odd)
    return first, second


def own_kernel(
    rows_ref, occupied_ref, virtual_ref, low_ref, high_ref, density_ref, share_ref, two_ref, done
):
    share = share_ref.shape[0]
    caps, pair_width = share_ref.shape[1:]
    first = pl.multiple_of(lax.axis_index("tm") * share, share)
    copies = [
        pltpu.make_async_copy(rows_ref.at[pl.ds(first, share)], share_ref, done.at[0]),
        pltpu.make_async_copy(occupied_ref.at[0, 0], two_ref.at[0], done.at[1]),
        pltpu.make_async_copy(virtual_ref.at[0, 0], two_ref.at[1], done.at[2]),
    ]
    for copy in copies:
        copy.start()
    for copy in copies[1:]:
        copy.wait()
    row = lax.broadcasted_iota(jnp.int32, (HALF, HALF), 0)
    col = lax.broadcasted_iota(jnp.int32, (HALF, HALF), 1)
    source = 2 * (col % (HALF // 2)) + col // (HALF // 2)
    order = (row == source).astype(jnp.float32).astype(jnp.bfloat16)
    turned = two_ref[0].astype(jnp.float32).T.astype(jnp.bfloat16)
    moved = jnp.dot(turned, order, preferred_element_type=jnp.float32)
    both = jnp.concatenate([moved, two_ref[1].astype(jnp.float32)], axis=1).astype(jnp.bfloat16)
    density_ref[...] = both
    half = share // 2
    for piece in range(HALF // half):
        place = caps * pair_width + piece * LANES
        block = both[piece * half : (piece + 1) * half]
        low_ref[:, place : place + LANES] = block
        high_ref[:, place : place + LANES] = block
    copies[0].wait()
    width = 1024
    for place in range(0, pair_width, width):
        apart = jnp.swapaxes(share_ref[:, :, place : place + width], 0, 1)
        for column in range(caps):
            lanes = slice(column * pair_width + place, column * pair_width + place + width)
            low_ref[:, lanes] = apart[column, :half]
            high_ref[:, lanes] = apart[column, half:]


def pair_kernel(low_ref, high_ref, x_ref, y_ref, *refs):
    to_x_ref, to_y_ref = refs[-2:]
    caps, pair_width = to_x_ref.shape[1], to_x_ref.shape[3]
    for column in range(caps):
        lanes = slice(column * pair_width, (column + 1) * pair_width)
        to_x_ref[0, column] = high_ref[:, lanes]
        to_x_ref[1, column] = y_ref[:, lanes]
        to_y_ref[0, column] = low_ref[:, lanes]
        to_y_ref[1, column] = x_ref[:, lanes]


def gather_kernel(density_ref, x_ref, y_ref, d_ref, out_ref):
    half = x_ref.shape[0]
    start = x_ref.shape[1] - HALF // half * LANES
    out_ref[0] = density_ref[...]
    out_ref[3] = d_ref[...]
    for piece in range(HALF // half):
        lanes = slice(start + piece * LANES, start + (piece + 1) * LANES)
        out_ref[1, piece * half : (piece + 1) * half] = x_ref[:, lanes]
        out_ref[2, piece * half : (piece + 1) * half] = y_ref[:, lanes]


def order_kernel(x_ref, y_ref, *refs):
    refs[-2][...] = x_ref[...]
    refs[-1][...] = y_ref[...]


def turn_kernel(rows_ref, out_ref, apart_ref):
    caps, parts, count, pair_width = out_ref.shape
    width = 1024
    for place in range(0, pair_width, width):
        block = rows_ref[:, :, place : place + width]
        apart_ref[:, :, place : place + width] = jnp.swapaxes(block, 0, 1)
    for column in range(caps):
        for part in range(parts):
            lanes = [
                apart_ref[column, part * count : (part + 1) * count, place : place + LANES]
                for place in range(0, pair_width, LANES)
            ]
            by_row = jnp.swapaxes(jnp.stack(lanes), 0, 1)
            for low in range(count // 2):
                first, second = exchange_halves(by_row[low], by_row[low + count // 2])
                place = slice(low * LANES, (low + 1) * LANES)
                out_ref[column, part, : count // 2, place] = first
                out_ref[column, part, count // 2 :, place] = second


def pick_kernel(lists_ref, near_ref, core_ref, after_ref, out_ref, all_ref):
    device = lax.axis_index("tensor")
    for move in range(4):
        all_ref[2 * move] = near_ref[move]
        all_ref[2 * move + 1] = core_ref[move]
    for column in range(out_ref.shape[0]):
        for part in range(out_ref.shape[1]):
            pair = lists_ref[column, 2 * device + part]
            out_ref[column, part] = all_ref[pair ^ device]


def mix_kernel(turned_ref, density_ref, out_ref, mark_ref):
    caps, parts, count, pair_width = out_ref.shape
    wide = 4 * HALF
    row_ids = lax.broadcasted_iota(jnp.int32, (wide, wide), 0) // HALF
    col_ids = lax.broadcasted_iota(jnp.int32, (wide, wide), 1) // HALF
    groups = pair_width // wide
    mark_ref[...] = jnp.zeros_like(mark_ref)
    for column in range(caps):
        for part in range(parts):
            occupied = density_ref[column, part, :, :HALF]
            virtual = density_ref[column, part, :, HALF:].astype(jnp.float32)
            twice = jnp.concatenate([virtual, virtual], axis=1)
            strip = jnp.concatenate([twice, twice], axis=1)
            tiled = jnp.concatenate([strip, strip, strip, strip], axis=0)
            diagonal = jnp.where(row_ids == col_ids, tiled, 0.0).astype(jnp.bfloat16)
            halves = []
            for group in range(groups):
                half_done = jnp.dot(
                    occupied,
                    turned_ref[column, part, :, group * wide : (group + 1) * wide],
                    preferred_element_type=jnp.float32,
                )
                halves.append(half_done.astype(jnp.bfloat16))
            mixed = jnp.dot(
                jnp.concatenate(halves, axis=0), diagonal, preferred_element_type=jnp.float32
            ).astype(jnp.bfloat16)
            near = mixed[:, :LANES].reshape(groups, HALF, LANES)
            far = mixed[:, LANES:].reshape(groups, HALF, LANES)
            by_row = jnp.stack([near, far], axis=1).reshape(2 * groups, HALF, LANES)
            by_row = jnp.swapaxes(by_row, 0, 1)
            for pair in range(HALF // 2):
                first, second = exchange_halves(by_row[2 * pair], by_row[2 * pair + 1])
                place = slice(pair * LANES, (pair + 1) * LANES)
                out_ref[column, part, : count // 2, place] = first
                out_ref[column, part, count // 2 :, place] = second


def gram_kernel(weights_ref, lists_ref, *refs):
    mixed_refs, near_refs, core_refs, out_ref = refs[:4], refs[4:8], refs[8:12], refs[12]
    plane = lax.axis_index("tm")
    device = lax.axis_index("tensor")
    caps = mixed_refs[0].shape[0]
    rows, columns = out_ref.shape[1:]
    owner = lax.broadcasted_iota(jnp.int32, (1, columns), 1) // (columns // 8)
    for part in range(rows // HALF):
        chi = [None] * 4
        for mine in range(caps):
            pair = lists_ref[mine, 2 * device + part]
            listed = jnp.zeros((1, columns), jnp.int32)
            right = []
            for move in range(8):
                block = 2 * (device ^ move) + plane // 2
                second = (lists_ref[1, block] == pair).astype(jnp.int32)
                either = second + (lists_ref[0, block] == pair).astype(jnp.int32)
                listed = jnp.where(owner == move, either, listed)
                to_x, to_y, from_x, from_y = core_refs if move % 2 else near_refs
                halves = (
                    (to_y.at[0], to_x.at[0]),
                    (to_y.at[1], from_x.at[0]),
                    (from_y.at[0], to_x.at[1]),
                    (from_y.at[1], from_x.at[1]),
                )[move // 2]
                right += [half[second] for half in halves]
            left = [mixed[mine, part] for mixed in mixed_refs]
            found = lax.dot_general(
                jnp.concatenate(left, axis=0),
                jnp.concatenate(right, axis=0),
                (((1,), (1,)), ((), ())),
                preferred_element_type=jnp.float32,
            )
            found = jnp.where(listed > 0, found, 0.0)
            for time in range(4):
                term = found[time * HALF : (time + 1) * HALF]
                chi[time] = term if chi[time] is None else chi[time] + term
        for freq in range(4):
            value = weights_ref[plane ^ freq, plane] * chi[0]
            for time in range(1, 4):
                value = value + weights_ref[plane ^ freq, plane ^ time] * chi[time]
            out_ref[freq, part * HALF : (part + 1) * HALF, :] = value.astype(out_ref.dtype)


def factor_kernel(factor_ref, out_ref):
    plane = lax.axis_index("tm")
    device = lax.axis_index("tensor")
    share = out_ref.shape[1] // 8
    out_ref[...] = jnp.zeros_like(out_ref)
    right = lax.broadcasted_iota(jnp.int32, (share, LANES), 1) // HALF
    for slot in range(4):
        other = plane ^ slot
        first = pl.multiple_of((other % 2) * share, share)
        for move in range(8):
            factor = factor_ref[2 * (device ^ move) + other // 2, pl.ds(first, share), :]
            wide = jnp.where(right == other // 2, jnp.concatenate([factor, factor], axis=1), 0.0)
            rows = slice(move * share, (move + 1) * share)
            out_ref[slot, rows, move * LANES : (move + 1) * LANES] = wide.astype(out_ref.dtype)


def screen_kernel(chi_ref, r3, r2, r1, factor_ref, out_ref, block_ref, done):
    device = lax.axis_index("tensor")
    sources = [chi_ref[0], r1[...], r2[...], r3[...]]
    copies = []
    for pair in range(4):
        lanes = slice(2 * pair * LANES, 2 * (pair + 1) * LANES)
        total = None
        for slot in range(4):
            term = jnp.dot(
                sources[slot], factor_ref[slot, :, lanes], preferred_element_type=jnp.float32
            )
            total = term if total is None else total + term
        for side in range(2):
            move = 2 * pair + side
            block_ref[move] = total[:, side * LANES : (side + 1) * LANES]
            place = pl.ds(pl.multiple_of((device ^ move) * LANES, LANES), LANES)
            copies.append(
                pltpu.make_async_copy(block_ref.at[move], out_ref.at[0, :, place], done.at[move])
            )
            copies[-1].start()
    for copy in copies:
        copy.wait()


def small_slice(integrals, pair_lists, occ_density, virt_density, cosine_weights, coulomb_blocks):
    local_count, caps, pair_width = integrals.shape
    share = local_count // 4
    columns = 8 * share
    vmem = pl.BlockSpec(memory_space=pltpu.VMEM)
    smem = pl.BlockSpec(memory_space=pltpu.SMEM)
    tiles = jax.ShapeDtypeStruct((caps, 2, HALF, pair_width), jnp.bfloat16)

    def kernel(body, out_shape, in_specs, microseconds, scratch=(), room=16, **options):
        options = {"out_specs": jax.tree.map(lambda _: vmem, out_shape), **options}
        return pl.pallas_call(
            body,
            out_shape=out_shape,
            in_specs=in_specs,
            scratch_shapes=list(scratch),
            compiler_params=pltpu.CompilerParams(vmem_limit_bytes=room * 1024 * 1024),
            cost_estimate=pl.CostEstimate(
                flops=int(microseconds * 1e9), bytes_accessed=0, transcendentals=0
            ),
            **options,
        )

    def across(array, move):
        return lax.ppermute(array, "tensor", [(i, i ^ move) for i in range(8)])

    def planes(array, move):
        return lax.ppermute(array, "tm", [(i, i ^ move) for i in range(4)])

    lists = pair_lists.T
    half = share // 2
    message = jax.ShapeDtypeStruct(
        (half, caps * pair_width + HALF // half * LANES), jnp.bfloat16
    )
    block = jax.ShapeDtypeStruct((HALF, LANES), jnp.bfloat16)
    both = jax.ShapeDtypeStruct((2, caps, half, pair_width), jnp.bfloat16)
    low, high, density = kernel(
        own_kernel,
        [message, message, block],
        [pl.BlockSpec(memory_space=pltpu.HBM)] * 3,
        2,
        [
            pltpu.VMEM((share, caps, pair_width), jnp.bfloat16),
            pltpu.VMEM((2, HALF, HALF), jnp.bfloat16),
            pltpu.SemaphoreType.DMA((3,)),
        ],
        room=61,
    )(integrals, occ_density, virt_density)
    x_low = across(low, 2)
    y_high = across(high, 4)
    turned = kernel(
        turn_kernel, tiles, [vmem], 1.2, [pltpu.VMEM((caps, local_count, pair_width), jnp.bfloat16)]
    )(integrals)
    near = kernel(
        gather_kernel, jax.ShapeDtypeStruct((4, HALF, LANES), jnp.bfloat16), [vmem] * 4, 0.2
    )(density, x_low, y_high, across(density, 6))
    factors = kernel(
        factor_kernel, jax.ShapeDtypeStruct((4, columns, 8 * LANES), jnp.bfloat16), [vmem], 1
    )(coulomb_blocks)
    to_x, to_y = kernel(pair_kernel, [both] * 2, [vmem] * 7, 0.3)(
        low, high, x_low, y_high, turned, near, factors
    )
    picked = kernel(
        pick_kernel,
        jax.ShapeDtypeStruct((caps, 2, HALF, LANES), jnp.bfloat16),
        [smem] + [vmem] * 3,
        1,
        [pltpu.VMEM((8, HALF, LANES), jnp.bfloat16)],
    )(lists, near, across(near, 1), to_x)
    per_time = [picked] + [planes(picked, move) for move in range(1, 4)]

    mark = jax.ShapeDtypeStruct((8, LANES), jnp.float32)
    mixed, marks = zip(
        *[kernel(mix_kernel, [tiles, mark], [vmem] * 2, 0.1)(turned, each) for each in per_time]
    )

    from_x, from_y = kernel(order_kernel, [both] * 2, [vmem] * 6, 0.3)(
        across(to_x, 2), across(to_y, 4), *marks[:3], per_time[3]
    )
    pieces = [to_x, to_y, from_x, from_y]
    chi = kernel(
        gram_kernel,
        jax.ShapeDtypeStruct((4, local_count, columns), jnp.bfloat16),
        [smem, smem] + [vmem] * 12,
        3,
    )(cosine_weights, lists, *mixed, *pieces, *[across(piece, 1) for piece in pieces])

    received = [planes(chi[move], move) for move in (3, 2, 1)]
    return kernel(
        screen_kernel,
        jax.ShapeDtypeStruct((1, local_count, 8 * LANES), jnp.float32),
        [vmem] * 5,
        1,
        [pltpu.VMEM((8, local_count, LANES), jnp.float32), pltpu.SemaphoreType.DMA((8,))],
        out_specs=pl.BlockSpec(memory_space=pltpu.HBM),
    )(chi, *received, factors)


def per_device(integrals, pair_lists, occ_density, virt_density, cosine_weights, coulomb_blocks):
    planned = (
        lax.axis_size("tm") == 4
        and lax.axis_size("tensor") == 8
        and integrals.shape == (2 * HALF, 2, HALF * HALF)
        and coulomb_blocks.shape == (16, HALF, HALF)
    )
    step = small_slice if planned else any_slice
    return step(integrals, pair_lists, occ_density, virt_density, cosine_weights, coulomb_blocks)


def solution(mesh):
    in_specs = (
        P("tensor", None, None),
        P(),
        P("tm", "tensor", None, None),
        P("tm", "tensor", None, None),
        P(),
        P(),
    )
    out_specs = P("tm", "tensor", None)
    return jax.shard_map(
        per_device, mesh=mesh, in_specs=in_specs, out_specs=out_specs, check_vma=False
    )
```

```python
import functools

import jax
import jax.numpy as jnp
from jax import lax
from jax.experimental import pallas as pl
from jax.experimental.pallas import tpu as pltpu
from jax.sharding import PartitionSpec as P

MOST = 6
HALF = 64
LANES = 128


def listed_blocks(pair_lists, pair_index):
    block_count = pair_lists.shape[0]
    member = jnp.any(pair_lists == pair_index, axis=1)
    positions = jnp.cumsum(member.astype(jnp.int32)) - 1
    slot_ids = jnp.arange(MOST, dtype=jnp.int32)
    matches = member[None, :] & (positions[None, :] == slot_ids[:, None])
    labels = jnp.arange(block_count, dtype=jnp.int32)
    located = jnp.sum(jnp.where(matches, labels[None, :], 0), axis=1)
    return jnp.where(jnp.any(matches, axis=1), located, block_count)


def density_product(row_data, occupied, virtual):
    row_count = row_data.shape[0]
    orbital_width = occupied.shape[0]
    half_done = jnp.dot(
        row_data.reshape(row_count * orbital_width, orbital_width),
        virtual,
        preferred_element_type=jnp.float32,
    )
    half_done = half_done.astype(jnp.bfloat16).reshape(row_count, orbital_width, orbital_width)
    contracted = jnp.einsum("rms,ml->rls", half_done, occupied, preferred_element_type=jnp.float32)
    return contracted.astype(jnp.bfloat16).reshape(row_count, orbital_width * orbital_width)


def pack_rows(local_rows, first_row, pair_lists, pair_count, block_rows):
    row_count = local_rows.shape[0]
    row_ids = first_row + jnp.arange(row_count, dtype=jnp.int32)
    targets = pair_lists[row_ids // block_rows]
    places = jnp.broadcast_to(jnp.arange(row_count, dtype=jnp.int32)[:, None], targets.shape)
    zero_buffer = jnp.zeros((pair_count, row_count, local_rows.shape[2]), local_rows.dtype)
    filled = zero_buffer.at[targets, places].set(local_rows)
    return filled.reshape(pair_count * row_count, local_rows.shape[2])


def any_slice(integrals, pair_lists, occ_density, virt_density, cosine_weights, coulomb_blocks):
    tensor_size = lax.axis_size("tensor")
    owner_pair = lax.axis_index("tensor")
    local_count = integrals.shape[0]
    slab_rows = local_count * tensor_size
    block_count = coulomb_blocks.shape[0]
    block_rows = coulomb_blocks.shape[1]
    occupied = occ_density[0, 0]
    virtual = virt_density[0, 0]
    chosen = listed_blocks(pair_lists, owner_pair)
    wanted = (
        chosen[:, None] * block_rows + jnp.arange(block_rows, dtype=jnp.int32)[None, :]
    ).reshape(-1)
    outgoing = pack_rows(integrals, owner_pair * local_count, pair_lists, tensor_size, block_rows)
    arrived = lax.all_to_all(outgoing, "tensor", split_axis=0, concat_axis=0, tiled=True)
    tile_rows = jnp.take(arrived, wanted, axis=0, mode="fill", fill_value=0)
    weighted = density_product(tile_rows, occupied, virtual)
    gram_block = lax.dot_general(
        weighted, tile_rows, (((1,), (1,)), ((), ())), preferred_element_type=jnp.float32
    )
    most_count = chosen.shape[0]
    block_ids = jnp.arange(block_count, dtype=jnp.int32)
    slot_ids = jnp.arange(most_count, dtype=jnp.int32)
    block_match = chosen[None, :] == block_ids[:, None]
    slot_of = jnp.sum(jnp.where(block_match, slot_ids[None, :], 0), axis=1)
    present = jnp.any(block_match, axis=1)
    slab_ids = jnp.arange(slab_rows, dtype=jnp.int32)
    row_block = slab_ids // block_rows
    source_row = jnp.where(
        present[row_block],
        slot_of[row_block] * block_rows + slab_ids % block_rows,
        most_count * block_rows,
    )
    rounded_terms = gram_block.astype(jnp.bfloat16)
    outgoing_terms = jnp.take(rounded_terms, source_row, axis=0, mode="fill", fill_value=0)
    arrived_terms = lax.all_to_all(
        outgoing_terms, "tensor", split_axis=0, concat_axis=0, tiled=True
    )
    received = arrived_terms.reshape(tensor_size, local_count, most_count, block_rows)
    every_chosen = jax.vmap(lambda pair_index: listed_blocks(pair_lists, pair_index))(
        jnp.arange(tensor_size, dtype=jnp.int32)
    )
    placement = (every_chosen[:, :, None] == block_ids[None, None, :]).astype(jnp.bfloat16)
    placed = jnp.einsum("srja,sjp->rpa", received, placement, preferred_element_type=jnp.float32)
    chi_rows = placed.reshape(local_count, slab_rows)
    spread = jnp.einsum(
        "ft,trc->frc",
        cosine_weights,
        lax.all_to_all(
            chi_rows[None].astype(jnp.bfloat16), "tm", split_axis=2, concat_axis=0, tiled=True
        ).astype(jnp.float32),
        precision=lax.Precision.HIGHEST,
    )
    freq_rows = lax.all_to_all(
        spread.astype(jnp.bfloat16), "tm", split_axis=0, concat_axis=2, tiled=True
    ).astype(spread.dtype)
    shaped = freq_rows.reshape(1, local_count, block_count, block_rows)
    screened = jnp.einsum("frpa,pab->frpb", shaped, coulomb_blocks, precision=lax.Precision.HIGHEST)
    return screened.reshape(1, local_count, slab_rows)


def exchange_halves(even, odd):
    left = lax.broadcasted_iota(jnp.int32, even.shape, 1) < HALF
    first = jnp.where(left, even, pltpu.roll(odd, HALF, 1))
    second = jnp.where(left, pltpu.roll(even, HALF, 1), odd)
    return first, second


def own_kernel(
    rows_ref, occupied_ref, virtual_ref, low_ref, high_ref, density_ref, share_ref, two_ref, done
):
    share = share_ref.shape[0]
    caps, pair_width = share_ref.shape[1:]
    first = pl.multiple_of(lax.axis_index("tm") * share, share)
    copies = [
        pltpu.make_async_copy(rows_ref.at[pl.ds(first, share)], share_ref, done.at[0]),
        pltpu.make_async_copy(occupied_ref.at[0, 0], two_ref.at[0], done.at[1]),
        pltpu.make_async_copy(virtual_ref.at[0, 0], two_ref.at[1], done.at[2]),
    ]
    for copy in copies:
        copy.start()
    for copy in copies[1:]:
        copy.wait()
    row = lax.broadcasted_iota(jnp.int32, (HALF, HALF), 0)
    col = lax.broadcasted_iota(jnp.int32, (HALF, HALF), 1)
    source = 2 * (col % (HALF // 2)) + col // (HALF // 2)
    order = (row == source).astype(jnp.float32).astype(jnp.bfloat16)
    turned = two_ref[0].astype(jnp.float32).T.astype(jnp.bfloat16)
    moved = jnp.dot(turned, order, preferred_element_type=jnp.float32)
    both = jnp.concatenate([moved, two_ref[1].astype(jnp.float32)], axis=1).astype(jnp.bfloat16)
    density_ref[...] = both
    half = share // 2
    for piece in range(HALF // half):
        place = caps * pair_width + piece * LANES
        block = both[piece * half : (piece + 1) * half]
        low_ref[:, place : place + LANES] = block
        high_ref[:, place : place + LANES] = block
    copies[0].wait()
    width = 1024
    for place in range(0, pair_width, width):
        apart = jnp.swapaxes(share_ref[:, :, place : place + width], 0, 1)
        for column in range(caps):
            lanes = slice(column * pair_width + place, column * pair_width + place + width)
            low_ref[:, lanes] = apart[column, :half]
            high_ref[:, lanes] = apart[column, half:]


def pair_kernel(low_ref, high_ref, x_ref, y_ref, *refs):
    to_x_ref, to_y_ref = refs[-2:]
    caps, pair_width = to_x_ref.shape[1], to_x_ref.shape[3]
    for column in range(caps):
        lanes = slice(column * pair_width, (column + 1) * pair_width)
        to_x_ref[0, column] = high_ref[:, lanes]
        to_x_ref[1, column] = y_ref[:, lanes]
        to_y_ref[0, column] = low_ref[:, lanes]
        to_y_ref[1, column] = x_ref[:, lanes]


def gather_kernel(density_ref, x_ref, y_ref, d_ref, out_ref):
    half = x_ref.shape[0]
    start = x_ref.shape[1] - HALF // half * LANES
    out_ref[0] = density_ref[...]
    out_ref[3] = d_ref[...]
    for piece in range(HALF // half):
        lanes = slice(start + piece * LANES, start + (piece + 1) * LANES)
        out_ref[1, piece * half : (piece + 1) * half] = x_ref[:, lanes]
        out_ref[2, piece * half : (piece + 1) * half] = y_ref[:, lanes]


def order_kernel(x_ref, y_ref, *refs):
    refs[-2][...] = x_ref[...]
    refs[-1][...] = y_ref[...]


def turn_kernel(rows_ref, out_ref, apart_ref):
    caps, parts, count, pair_width = out_ref.shape
    width = 1024
    for place in range(0, pair_width, width):
        block = rows_ref[:, :, place : place + width]
        apart_ref[:, :, place : place + width] = jnp.swapaxes(block, 0, 1)
    for column in range(caps):
        for part in range(parts):
            lanes = [
                apart_ref[column, part * count : (part + 1) * count, place : place + LANES]
                for place in range(0, pair_width, LANES)
            ]
            by_row = jnp.swapaxes(jnp.stack(lanes), 0, 1)
            for low in range(count // 2):
                first, second = exchange_halves(by_row[low], by_row[low + count // 2])
                place = slice(low * LANES, (low + 1) * LANES)
                out_ref[column, part, : count // 2, place] = first
                out_ref[column, part, count // 2 :, place] = second


def pick_kernel(lists_ref, near_ref, core_ref, after_ref, out_ref, all_ref):
    device = lax.axis_index("tensor")
    for move in range(4):
        all_ref[2 * move] = near_ref[move]
        all_ref[2 * move + 1] = core_ref[move]
    for column in range(out_ref.shape[0]):
        for part in range(out_ref.shape[1]):
            pair = lists_ref[column, 2 * device + part]
            out_ref[column, part] = all_ref[pair ^ device]


def mix_kernel(turned_ref, density_ref, out_ref, mark_ref):
    caps, parts, count, pair_width = out_ref.shape
    wide = 4 * HALF
    row_ids = lax.broadcasted_iota(jnp.int32, (wide, wide), 0) // HALF
    col_ids = lax.broadcasted_iota(jnp.int32, (wide, wide), 1) // HALF
    groups = pair_width // wide
    mark_ref[...] = jnp.zeros_like(mark_ref)
    for column in range(caps):
        for part in range(parts):
            occupied = density_ref[column, part, :, :HALF]
            virtual = density_ref[column, part, :, HALF:].astype(jnp.float32)
            twice = jnp.concatenate([virtual, virtual], axis=1)
            strip = jnp.concatenate([twice, twice], axis=1)
            tiled = jnp.concatenate([strip, strip, strip, strip], axis=0)
            diagonal = jnp.where(row_ids == col_ids, tiled, 0.0).astype(jnp.bfloat16)
            halves = []
            for group in range(groups):
                half_done = jnp.dot(
                    occupied,
                    turned_ref[column, part, :, group * wide : (group + 1) * wide],
                    preferred_element_type=jnp.float32,
                )
                halves.append(half_done.astype(jnp.bfloat16))
            mixed = jnp.dot(
                jnp.concatenate(halves, axis=0), diagonal, preferred_element_type=jnp.float32
            ).astype(jnp.bfloat16)
            near = mixed[:, :LANES].reshape(groups, HALF, LANES)
            far = mixed[:, LANES:].reshape(groups, HALF, LANES)
            by_row = jnp.stack([near, far], axis=1).reshape(2 * groups, HALF, LANES)
            by_row = jnp.swapaxes(by_row, 0, 1)
            for pair in range(HALF // 2):
                first, second = exchange_halves(by_row[2 * pair], by_row[2 * pair + 1])
                place = slice(pair * LANES, (pair + 1) * LANES)
                out_ref[column, part, : count // 2, place] = first
                out_ref[column, part, count // 2 :, place] = second


def gram_kernel(weights_ref, lists_ref, *refs):
    mixed_refs, near_refs, core_refs, out_ref = refs[:4], refs[4:8], refs[8:12], refs[12]
    plane = lax.axis_index("tm")
    device = lax.axis_index("tensor")
    caps = mixed_refs[0].shape[0]
    rows, columns = out_ref.shape[1:]
    owner = lax.broadcasted_iota(jnp.int32, (1, columns), 1) // (columns // 8)
    for part in range(rows // HALF):
        chi = [None] * 4
        for mine in range(caps):
            pair = lists_ref[mine, 2 * device + part]
            listed = jnp.zeros((1, columns), jnp.int32)
            right = []
            for move in range(8):
                block = 2 * (device ^ move) + plane // 2
                second = (lists_ref[1, block] == pair).astype(jnp.int32)
                either = second + (lists_ref[0, block] == pair).astype(jnp.int32)
                listed = jnp.where(owner == move, either, listed)
                to_x, to_y, from_x, from_y = core_refs if move % 2 else near_refs
                halves = (
                    (to_y.at[0], to_x.at[0]),
                    (to_y.at[1], from_x.at[0]),
                    (from_y.at[0], to_x.at[1]),
                    (from_y.at[1], from_x.at[1]),
                )[move // 2]
                right += [half[second] for half in halves]
            left = [mixed[mine, part] for mixed in mixed_refs]
            found = lax.dot_general(
                jnp.concatenate(left, axis=0),
                jnp.concatenate(right, axis=0),
                (((1,), (1,)), ((), ())),
                preferred_element_type=jnp.float32,
            )
            found = jnp.where(listed > 0, found, 0.0)
            for time in range(4):
                term = found[time * HALF : (time + 1) * HALF]
                chi[time] = term if chi[time] is None else chi[time] + term
        for freq in range(4):
            value = weights_ref[plane ^ freq, plane] * chi[0]
            for time in range(1, 4):
                value = value + weights_ref[plane ^ freq, plane ^ time] * chi[time]
            out_ref[freq, part * HALF : (part + 1) * HALF, :] = value.astype(out_ref.dtype)


def factor_kernel(factor_ref, out_ref):
    plane = lax.axis_index("tm")
    device = lax.axis_index("tensor")
    share = out_ref.shape[1] // 8
    out_ref[...] = jnp.zeros_like(out_ref)
    right = lax.broadcasted_iota(jnp.int32, (share, LANES), 1) // HALF
    for slot in range(4):
        other = plane ^ slot
        first = pl.multiple_of((other % 2) * share, share)
        for move in range(8):
            factor = factor_ref[2 * (device ^ move) + other // 2, pl.ds(first, share), :]
            wide = jnp.where(right == other // 2, jnp.concatenate([factor, factor], axis=1), 0.0)
            rows = slice(move * share, (move + 1) * share)
            out_ref[slot, rows, move * LANES : (move + 1) * LANES] = wide.astype(out_ref.dtype)


def screen_kernel(chi_ref, r3, r2, r1, factor_ref, out_ref, block_ref, done):
    device = lax.axis_index("tensor")
    sources = [chi_ref[0], r1[...], r2[...], r3[...]]
    copies = []
    for pair in range(4):
        lanes = slice(2 * pair * LANES, 2 * (pair + 1) * LANES)
        total = None
        for slot in range(4):
            term = jnp.dot(
                sources[slot], factor_ref[slot, :, lanes], preferred_element_type=jnp.float32
            )
            total = term if total is None else total + term
        for side in range(2):
            move = 2 * pair + side
            block_ref[move] = total[:, side * LANES : (side + 1) * LANES]
            place = pl.ds(pl.multiple_of((device ^ move) * LANES, LANES), LANES)
            copies.append(
                pltpu.make_async_copy(block_ref.at[move], out_ref.at[0, :, place], done.at[move])
            )
            copies[-1].start()
    for copy in copies:
        copy.wait()


def small_slice(integrals, pair_lists, occ_density, virt_density, cosine_weights, coulomb_blocks):
    local_count, caps, pair_width = integrals.shape
    share = local_count // 4
    columns = 8 * share
    vmem = pl.BlockSpec(memory_space=pltpu.VMEM)
    smem = pl.BlockSpec(memory_space=pltpu.SMEM)
    tiles = jax.ShapeDtypeStruct((caps, 2, HALF, pair_width), jnp.bfloat16)

    def kernel(body, out_shape, in_specs, microseconds, scratch=(), room=16, **options):
        options = {"out_specs": jax.tree.map(lambda _: vmem, out_shape), **options}
        return pl.pallas_call(
            body,
            out_shape=out_shape,
            in_specs=in_specs,
            scratch_shapes=list(scratch),
            compiler_params=pltpu.CompilerParams(vmem_limit_bytes=room * 1024 * 1024),
            cost_estimate=pl.CostEstimate(
                flops=int(microseconds * 1e9), bytes_accessed=0, transcendentals=0
            ),
            **options,
        )

    def across(array, move):
        return lax.ppermute(array, "tensor", [(i, i ^ move) for i in range(8)])

    def planes(array, move):
        return lax.ppermute(array, "tm", [(i, i ^ move) for i in range(4)])

    lists = pair_lists.T
    half = share // 2
    message = jax.ShapeDtypeStruct(
        (half, caps * pair_width + HALF // half * LANES), jnp.bfloat16
    )
    block = jax.ShapeDtypeStruct((HALF, LANES), jnp.bfloat16)
    both = jax.ShapeDtypeStruct((2, caps, half, pair_width), jnp.bfloat16)
    low, high, density = kernel(
        own_kernel,
        [message, message, block],
        [pl.BlockSpec(memory_space=pltpu.HBM)] * 3,
        2,
        [
            pltpu.VMEM((share, caps, pair_width), jnp.bfloat16),
            pltpu.VMEM((2, HALF, HALF), jnp.bfloat16),
            pltpu.SemaphoreType.DMA((3,)),
        ],
        room=62,
    )(integrals, occ_density, virt_density)
    x_low = across(low, 2)
    y_high = across(high, 4)
    turned = kernel(
        turn_kernel, tiles, [vmem], 1.2, [pltpu.VMEM((caps, local_count, pair_width), jnp.bfloat16)]
    )(integrals)
    near = kernel(
        gather_kernel, jax.ShapeDtypeStruct((4, HALF, LANES), jnp.bfloat16), [vmem] * 4, 0.2
    )(density, x_low, y_high, across(density, 6))
    factors = kernel(
        factor_kernel, jax.ShapeDtypeStruct((4, columns, 8 * LANES), jnp.bfloat16), [vmem], 1
    )(coulomb_blocks)
    to_x, to_y = kernel(pair_kernel, [both] * 2, [vmem] * 7, 0.3)(
        low, high, x_low, y_high, turned, near, factors
    )
    picked = kernel(
        pick_kernel,
        jax.ShapeDtypeStruct((caps, 2, HALF, LANES), jnp.bfloat16),
        [smem] + [vmem] * 3,
        1,
        [pltpu.VMEM((8, HALF, LANES), jnp.bfloat16)],
    )(lists, near, across(near, 1), to_x)
    per_time = [picked] + [planes(picked, move) for move in range(1, 4)]

    mark = jax.ShapeDtypeStruct((8, LANES), jnp.float32)
    mixed, marks = zip(
        *[kernel(mix_kernel, [tiles, mark], [vmem] * 2, 0.1)(turned, each) for each in per_time]
    )

    from_x, from_y = kernel(order_kernel, [both] * 2, [vmem] * 6, 0.3)(
        across(to_x, 2), across(to_y, 4), *marks[:3], per_time[3]
    )
    pieces = [to_x, to_y, from_x, from_y]
    chi = kernel(
        gram_kernel,
        jax.ShapeDtypeStruct((4, local_count, columns), jnp.bfloat16),
        [smem, smem] + [vmem] * 12,
        3,
    )(cosine_weights, lists, *mixed, *pieces, *[across(piece, 1) for piece in pieces])

    received = [planes(chi[move], move) for move in (3, 2, 1)]
    return kernel(
        screen_kernel,
        jax.ShapeDtypeStruct((1, local_count, 8 * LANES), jnp.float32),
        [vmem] * 5,
        1,
        [pltpu.VMEM((8, local_count, LANES), jnp.float32), pltpu.SemaphoreType.DMA((8,))],
        out_specs=pl.BlockSpec(memory_space=pltpu.HBM),
    )(chi, *received, factors)


def per_device(integrals, pair_lists, occ_density, virt_density, cosine_weights, coulomb_blocks):
    planned = (
        lax.axis_size("tm") == 4
        and lax.axis_size("tensor") == 8
        and integrals.shape == (2 * HALF, 2, HALF * HALF)
        and coulomb_blocks.shape == (16, HALF, HALF)
    )
    step = small_slice if planned else any_slice
    return step(integrals, pair_lists, occ_density, virt_density, cosine_weights, coulomb_blocks)


def solution(mesh):
    in_specs = (
        P("tensor", None, None),
        P(),
        P("tm", "tensor", None, None),
        P("tm", "tensor", None, None),
        P(),
        P(),
    )
    out_specs = P("tm", "tensor", None)
    return jax.shard_map(
        per_device, mesh=mesh, in_specs=in_specs, out_specs=out_specs, check_vma=False
    )
```

```python
import functools

import jax
import jax.numpy as jnp
from jax import lax
from jax.experimental import pallas as pl
from jax.experimental.pallas import tpu as pltpu
from jax.sharding import PartitionSpec as P

MOST = 6
HALF = 64
LANES = 128


def listed_blocks(pair_lists, pair_index):
    block_count = pair_lists.shape[0]
    member = jnp.any(pair_lists == pair_index, axis=1)
    positions = jnp.cumsum(member.astype(jnp.int32)) - 1
    slot_ids = jnp.arange(MOST, dtype=jnp.int32)
    matches = member[None, :] & (positions[None, :] == slot_ids[:, None])
    labels = jnp.arange(block_count, dtype=jnp.int32)
    located = jnp.sum(jnp.where(matches, labels[None, :], 0), axis=1)
    return jnp.where(jnp.any(matches, axis=1), located, block_count)


def density_product(row_data, occupied, virtual):
    row_count = row_data.shape[0]
    orbital_width = occupied.shape[0]
    half_done = jnp.dot(
        row_data.reshape(row_count * orbital_width, orbital_width),
        virtual,
        preferred_element_type=jnp.float32,
    )
    half_done = half_done.astype(jnp.bfloat16).reshape(row_count, orbital_width, orbital_width)
    contracted = jnp.einsum("rms,ml->rls", half_done, occupied, preferred_element_type=jnp.float32)
    return contracted.astype(jnp.bfloat16).reshape(row_count, orbital_width * orbital_width)


def pack_rows(local_rows, first_row, pair_lists, pair_count, block_rows):
    row_count = local_rows.shape[0]
    row_ids = first_row + jnp.arange(row_count, dtype=jnp.int32)
    targets = pair_lists[row_ids // block_rows]
    places = jnp.broadcast_to(jnp.arange(row_count, dtype=jnp.int32)[:, None], targets.shape)
    zero_buffer = jnp.zeros((pair_count, row_count, local_rows.shape[2]), local_rows.dtype)
    filled = zero_buffer.at[targets, places].set(local_rows)
    return filled.reshape(pair_count * row_count, local_rows.shape[2])


def any_slice(integrals, pair_lists, occ_density, virt_density, cosine_weights, coulomb_blocks):
    tensor_size = lax.axis_size("tensor")
    owner_pair = lax.axis_index("tensor")
    local_count = integrals.shape[0]
    slab_rows = local_count * tensor_size
    block_count = coulomb_blocks.shape[0]
    block_rows = coulomb_blocks.shape[1]
    occupied = occ_density[0, 0]
    virtual = virt_density[0, 0]
    chosen = listed_blocks(pair_lists, owner_pair)
    wanted = (
        chosen[:, None] * block_rows + jnp.arange(block_rows, dtype=jnp.int32)[None, :]
    ).reshape(-1)
    outgoing = pack_rows(integrals, owner_pair * local_count, pair_lists, tensor_size, block_rows)
    arrived = lax.all_to_all(outgoing, "tensor", split_axis=0, concat_axis=0, tiled=True)
    tile_rows = jnp.take(arrived, wanted, axis=0, mode="fill", fill_value=0)
    weighted = density_product(tile_rows, occupied, virtual)
    gram_block = lax.dot_general(
        weighted, tile_rows, (((1,), (1,)), ((), ())), preferred_element_type=jnp.float32
    )
    most_count = chosen.shape[0]
    block_ids = jnp.arange(block_count, dtype=jnp.int32)
    slot_ids = jnp.arange(most_count, dtype=jnp.int32)
    block_match = chosen[None, :] == block_ids[:, None]
    slot_of = jnp.sum(jnp.where(block_match, slot_ids[None, :], 0), axis=1)
    present = jnp.any(block_match, axis=1)
    slab_ids = jnp.arange(slab_rows, dtype=jnp.int32)
    row_block = slab_ids // block_rows
    source_row = jnp.where(
        present[row_block],
        slot_of[row_block] * block_rows + slab_ids % block_rows,
        most_count * block_rows,
    )
    rounded_terms = gram_block.astype(jnp.bfloat16)
    outgoing_terms = jnp.take(rounded_terms, source_row, axis=0, mode="fill", fill_value=0)
    arrived_terms = lax.all_to_all(
        outgoing_terms, "tensor", split_axis=0, concat_axis=0, tiled=True
    )
    received = arrived_terms.reshape(tensor_size, local_count, most_count, block_rows)
    every_chosen = jax.vmap(lambda pair_index: listed_blocks(pair_lists, pair_index))(
        jnp.arange(tensor_size, dtype=jnp.int32)
    )
    placement = (every_chosen[:, :, None] == block_ids[None, None, :]).astype(jnp.bfloat16)
    placed = jnp.einsum("srja,sjp->rpa", received, placement, preferred_element_type=jnp.float32)
    chi_rows = placed.reshape(local_count, slab_rows)
    spread = jnp.einsum(
        "ft,trc->frc",
        cosine_weights,
        lax.all_to_all(
            chi_rows[None].astype(jnp.bfloat16), "tm", split_axis=2, concat_axis=0, tiled=True
        ).astype(jnp.float32),
        precision=lax.Precision.HIGHEST,
    )
    freq_rows = lax.all_to_all(
        spread.astype(jnp.bfloat16), "tm", split_axis=0, concat_axis=2, tiled=True
    ).astype(spread.dtype)
    shaped = freq_rows.reshape(1, local_count, block_count, block_rows)
    screened = jnp.einsum("frpa,pab->frpb", shaped, coulomb_blocks, precision=lax.Precision.HIGHEST)
    return screened.reshape(1, local_count, slab_rows)


def exchange_halves(even, odd):
    left = lax.broadcasted_iota(jnp.int32, even.shape, 1) < HALF
    first = jnp.where(left, even, pltpu.roll(odd, HALF, 1))
    second = jnp.where(left, pltpu.roll(even, HALF, 1), odd)
    return first, second


def own_kernel(
    rows_ref, occupied_ref, virtual_ref, low_ref, high_ref, density_ref, share_ref, two_ref, done
):
    share = share_ref.shape[0]
    caps, pair_width = share_ref.shape[1:]
    first = pl.multiple_of(lax.axis_index("tm") * share, share)
    copies = [
        pltpu.make_async_copy(rows_ref.at[pl.ds(first, share)], share_ref, done.at[0]),
        pltpu.make_async_copy(occupied_ref.at[0, 0], two_ref.at[0], done.at[1]),
        pltpu.make_async_copy(virtual_ref.at[0, 0], two_ref.at[1], done.at[2]),
    ]
    for copy in copies:
        copy.start()
    for copy in copies[1:]:
        copy.wait()
    row = lax.broadcasted_iota(jnp.int32, (HALF, HALF), 0)
    col = lax.broadcasted_iota(jnp.int32, (HALF, HALF), 1)
    source = 2 * (col % (HALF // 2)) + col // (HALF // 2)
    order = (row == source).astype(jnp.float32).astype(jnp.bfloat16)
    turned = two_ref[0].astype(jnp.float32).T.astype(jnp.bfloat16)
    moved = jnp.dot(turned, order, preferred_element_type=jnp.float32)
    both = jnp.concatenate([moved, two_ref[1].astype(jnp.float32)], axis=1).astype(jnp.bfloat16)
    density_ref[...] = both
    half = share // 2
    for piece in range(HALF // half):
        place = caps * pair_width + piece * LANES
        block = both[piece * half : (piece + 1) * half]
        low_ref[:, place : place + LANES] = block
        high_ref[:, place : place + LANES] = block
    copies[0].wait()
    width = 1024
    for place in range(0, pair_width, width):
        apart = jnp.swapaxes(share_ref[:, :, place : place + width], 0, 1)
        for column in range(caps):
            lanes = slice(column * pair_width + place, column * pair_width + place + width)
            low_ref[:, lanes] = apart[column, :half]
            high_ref[:, lanes] = apart[column, half:]


def pair_kernel(low_ref, high_ref, x_ref, y_ref, *refs):
    to_x_ref, to_y_ref = refs[-2:]
    caps, pair_width = to_x_ref.shape[1], to_x_ref.shape[3]
    for column in range(caps):
        lanes = slice(column * pair_width, (column + 1) * pair_width)
        to_x_ref[0, column] = high_ref[:, lanes]
        to_x_ref[1, column] = y_ref[:, lanes]
        to_y_ref[0, column] = low_ref[:, lanes]
        to_y_ref[1, column] = x_ref[:, lanes]


def gather_kernel(density_ref, x_ref, y_ref, d_ref, out_ref):
    half = x_ref.shape[0]
    start = x_ref.shape[1] - HALF // half * LANES
    out_ref[0] = density_ref[...]
    out_ref[3] = d_ref[...]
    for piece in range(HALF // half):
        lanes = slice(start + piece * LANES, start + (piece + 1) * LANES)
        out_ref[1, piece * half : (piece + 1) * half] = x_ref[:, lanes]
        out_ref[2, piece * half : (piece + 1) * half] = y_ref[:, lanes]


def order_kernel(x_ref, y_ref, *refs):
    refs[-2][...] = x_ref[...]
    refs[-1][...] = y_ref[...]


def turn_kernel(rows_ref, out_ref, apart_ref):
    caps, parts, count, pair_width = out_ref.shape
    width = 1024
    for place in range(0, pair_width, width):
        block = rows_ref[:, :, place : place + width]
        apart_ref[:, :, place : place + width] = jnp.swapaxes(block, 0, 1)
    for column in range(caps):
        for part in range(parts):
            lanes = [
                apart_ref[column, part * count : (part + 1) * count, place : place + LANES]
                for place in range(0, pair_width, LANES)
            ]
            by_row = jnp.swapaxes(jnp.stack(lanes), 0, 1)
            for low in range(count // 2):
                first, second = exchange_halves(by_row[low], by_row[low + count // 2])
                place = slice(low * LANES, (low + 1) * LANES)
                out_ref[column, part, : count // 2, place] = first
                out_ref[column, part, count // 2 :, place] = second


def pick_kernel(lists_ref, near_ref, core_ref, after_ref, out_ref, all_ref):
    device = lax.axis_index("tensor")
    for move in range(4):
        all_ref[2 * move] = near_ref[move]
        all_ref[2 * move + 1] = core_ref[move]
    for column in range(out_ref.shape[0]):
        for part in range(out_ref.shape[1]):
            pair = lists_ref[column, 2 * device + part]
            out_ref[column, part] = all_ref[pair ^ device]


def mix_kernel(turned_ref, density_ref, out_ref, mark_ref):
    caps, parts, count, pair_width = out_ref.shape
    wide = 4 * HALF
    row_ids = lax.broadcasted_iota(jnp.int32, (wide, wide), 0) // HALF
    col_ids = lax.broadcasted_iota(jnp.int32, (wide, wide), 1) // HALF
    groups = pair_width // wide
    mark_ref[...] = jnp.zeros_like(mark_ref)
    for column in range(caps):
        for part in range(parts):
            occupied = density_ref[column, part, :, :HALF]
            virtual = density_ref[column, part, :, HALF:].astype(jnp.float32)
            twice = jnp.concatenate([virtual, virtual], axis=1)
            strip = jnp.concatenate([twice, twice], axis=1)
            tiled = jnp.concatenate([strip, strip, strip, strip], axis=0)
            diagonal = jnp.where(row_ids == col_ids, tiled, 0.0).astype(jnp.bfloat16)
            halves = []
            for group in range(groups):
                half_done = jnp.dot(
                    occupied,
                    turned_ref[column, part, :, group * wide : (group + 1) * wide],
                    preferred_element_type=jnp.float32,
                )
                halves.append(half_done.astype(jnp.bfloat16))
            mixed = jnp.dot(
                jnp.concatenate(halves, axis=0), diagonal, preferred_element_type=jnp.float32
            ).astype(jnp.bfloat16)
            near = mixed[:, :LANES].reshape(groups, HALF, LANES)
            far = mixed[:, LANES:].reshape(groups, HALF, LANES)
            by_row = jnp.stack([near, far], axis=1).reshape(2 * groups, HALF, LANES)
            by_row = jnp.swapaxes(by_row, 0, 1)
            for pair in range(HALF // 2):
                first, second = exchange_halves(by_row[2 * pair], by_row[2 * pair + 1])
                place = slice(pair * LANES, (pair + 1) * LANES)
                out_ref[column, part, : count // 2, place] = first
                out_ref[column, part, count // 2 :, place] = second


def gram_kernel(weights_ref, lists_ref, *refs):
    mixed_refs, near_refs, core_refs, out_ref = refs[:4], refs[4:8], refs[8:12], refs[12]
    plane = lax.axis_index("tm")
    device = lax.axis_index("tensor")
    caps = mixed_refs[0].shape[0]
    rows, columns = out_ref.shape[1:]
    owner = lax.broadcasted_iota(jnp.int32, (1, columns), 1) // (columns // 8)
    for part in range(rows // HALF):
        chi = [None] * 4
        for mine in range(caps):
            pair = lists_ref[mine, 2 * device + part]
            listed = jnp.zeros((1, columns), jnp.int32)
            right = []
            for move in range(8):
                block = 2 * (device ^ move) + plane // 2
                second = (lists_ref[1, block] == pair).astype(jnp.int32)
                either = second + (lists_ref[0, block] == pair).astype(jnp.int32)
                listed = jnp.where(owner == move, either, listed)
                to_x, to_y, from_x, from_y = core_refs if move % 2 else near_refs
                halves = (
                    (to_y.at[0], to_x.at[0]),
                    (to_y.at[1], from_x.at[0]),
                    (from_y.at[0], to_x.at[1]),
                    (from_y.at[1], from_x.at[1]),
                )[move // 2]
                right += [half[second] for half in halves]
            left = [mixed[mine, part] for mixed in mixed_refs]
            found = lax.dot_general(
                jnp.concatenate(left, axis=0),
                jnp.concatenate(right, axis=0),
                (((1,), (1,)), ((), ())),
                preferred_element_type=jnp.float32,
            )
            found = jnp.where(listed > 0, found, 0.0)
            for time in range(4):
                term = found[time * HALF : (time + 1) * HALF]
                chi[time] = term if chi[time] is None else chi[time] + term
        for freq in range(4):
            value = weights_ref[plane ^ freq, plane] * chi[0]
            for time in range(1, 4):
                value = value + weights_ref[plane ^ freq, plane ^ time] * chi[time]
            out_ref[freq, part * HALF : (part + 1) * HALF, :] = value.astype(out_ref.dtype)


def factor_kernel(factor_ref, out_ref):
    plane = lax.axis_index("tm")
    device = lax.axis_index("tensor")
    share = out_ref.shape[1] // 8
    out_ref[...] = jnp.zeros_like(out_ref)
    right = lax.broadcasted_iota(jnp.int32, (share, LANES), 1) // HALF
    for slot in range(4):
        other = plane ^ slot
        first = pl.multiple_of((other % 2) * share, share)
        for move in range(8):
            factor = factor_ref[2 * (device ^ move) + other // 2, pl.ds(first, share), :]
            wide = jnp.where(right == other // 2, jnp.concatenate([factor, factor], axis=1), 0.0)
            rows = slice(move * share, (move + 1) * share)
            out_ref[slot, rows, move * LANES : (move + 1) * LANES] = wide.astype(out_ref.dtype)


def screen_kernel(chi_ref, r3, r2, r1, factor_ref, out_ref, block_ref, done):
    device = lax.axis_index("tensor")
    sources = [chi_ref[0], r1[...], r2[...], r3[...]]
    copies = []
    for pair in range(4):
        lanes = slice(2 * pair * LANES, 2 * (pair + 1) * LANES)
        total = None
        for slot in range(4):
            term = jnp.dot(
                sources[slot], factor_ref[slot, :, lanes], preferred_element_type=jnp.float32
            )
            total = term if total is None else total + term
        for side in range(2):
            move = 2 * pair + side
            block_ref[move] = total[:, side * LANES : (side + 1) * LANES]
            place = pl.ds(pl.multiple_of((device ^ move) * LANES, LANES), LANES)
            copies.append(
                pltpu.make_async_copy(block_ref.at[move], out_ref.at[0, :, place], done.at[move])
            )
            copies[-1].start()
    for copy in copies:
        copy.wait()


def small_slice(integrals, pair_lists, occ_density, virt_density, cosine_weights, coulomb_blocks):
    local_count, caps, pair_width = integrals.shape
    share = local_count // 4
    columns = 8 * share
    vmem = pl.BlockSpec(memory_space=pltpu.VMEM)
    smem = pl.BlockSpec(memory_space=pltpu.SMEM)
    tiles = jax.ShapeDtypeStruct((caps, 2, HALF, pair_width), jnp.bfloat16)

    def kernel(body, out_shape, in_specs, microseconds, scratch=(), room=16, **options):
        options = {"out_specs": jax.tree.map(lambda _: vmem, out_shape), **options}
        return pl.pallas_call(
            body,
            out_shape=out_shape,
            in_specs=in_specs,
            scratch_shapes=list(scratch),
            compiler_params=pltpu.CompilerParams(vmem_limit_bytes=room * 1024 * 1024),
            cost_estimate=pl.CostEstimate(
                flops=int(microseconds * 1e9), bytes_accessed=0, transcendentals=0
            ),
            **options,
        )

    def across(array, move):
        return lax.ppermute(array, "tensor", [(i, i ^ move) for i in range(8)])

    def planes(array, move):
        return lax.ppermute(array, "tm", [(i, i ^ move) for i in range(4)])

    lists = pair_lists.T
    half = share // 2
    message = jax.ShapeDtypeStruct(
        (half, caps * pair_width + HALF // half * LANES), jnp.bfloat16
    )
    block = jax.ShapeDtypeStruct((HALF, LANES), jnp.bfloat16)
    both = jax.ShapeDtypeStruct((2, caps, half, pair_width), jnp.bfloat16)
    low, high, density = kernel(
        own_kernel,
        [message, message, block],
        [pl.BlockSpec(memory_space=pltpu.HBM)] * 3,
        2,
        [
            pltpu.VMEM((share, caps, pair_width), jnp.bfloat16),
            pltpu.VMEM((2, HALF, HALF), jnp.bfloat16),
            pltpu.SemaphoreType.DMA((3,)),
        ],
        room=62,
    )(integrals, occ_density, virt_density)
    x_low = across(low, 2)
    y_high = across(high, 4)
    turned = kernel(
        turn_kernel, tiles, [vmem], 1.2, [pltpu.VMEM((caps, local_count, pair_width), jnp.bfloat16)]
    )(integrals)
    near = kernel(
        gather_kernel, jax.ShapeDtypeStruct((4, HALF, LANES), jnp.bfloat16), [vmem] * 4, 0.2
    )(density, x_low, y_high, across(density, 6))
    factors = kernel(
        factor_kernel, jax.ShapeDtypeStruct((4, columns, 8 * LANES), jnp.bfloat16), [vmem], 1
    )(coulomb_blocks)
    to_x, to_y = kernel(pair_kernel, [both] * 2, [vmem] * 7, 0.3)(
        low, high, x_low, y_high, turned, near, factors
    )
    picked = kernel(
        pick_kernel,
        jax.ShapeDtypeStruct((caps, 2, HALF, LANES), jnp.bfloat16),
        [smem] + [vmem] * 3,
        1,
        [pltpu.VMEM((8, HALF, LANES), jnp.bfloat16)],
    )(lists, near, across(near, 1), to_x)
    per_time = [picked] + [planes(picked, move) for move in range(1, 4)]

    mark = jax.ShapeDtypeStruct((8, LANES), jnp.float32)
    mixed, marks = zip(
        *[kernel(mix_kernel, [tiles, mark], [vmem] * 2, 0.1)(turned, each) for each in per_time]
    )

    from_x, from_y = kernel(order_kernel, [both] * 2, [vmem] * 7, 0.3)(
        across(to_x, 2), across(to_y, 4), per_time[3], per_time[2], *marks[:3]
    )
    pieces = [to_x, to_y, from_x, from_y]
    chi = kernel(
        gram_kernel,
        jax.ShapeDtypeStruct((4, local_count, columns), jnp.bfloat16),
        [smem, smem] + [vmem] * 12,
        3,
    )(cosine_weights, lists, *mixed, *pieces, *[across(piece, 1) for piece in pieces])

    received = [planes(chi[move], move) for move in (3, 2, 1)]
    return kernel(
        screen_kernel,
        jax.ShapeDtypeStruct((1, local_count, 8 * LANES), jnp.float32),
        [vmem] * 5,
        1,
        [pltpu.VMEM((8, local_count, LANES), jnp.float32), pltpu.SemaphoreType.DMA((8,))],
        out_specs=pl.BlockSpec(memory_space=pltpu.HBM),
    )(chi, *received, factors)


def per_device(integrals, pair_lists, occ_density, virt_density, cosine_weights, coulomb_blocks):
    planned = (
        lax.axis_size("tm") == 4
        and lax.axis_size("tensor") == 8
        and integrals.shape == (2 * HALF, 2, HALF * HALF)
        and coulomb_blocks.shape == (16, HALF, HALF)
    )
    step = small_slice if planned else any_slice
    return step(integrals, pair_lists, occ_density, virt_density, cosine_weights, coulomb_blocks)


def solution(mesh):
    in_specs = (
        P("tensor", None, None),
        P(),
        P("tm", "tensor", None, None),
        P("tm", "tensor", None, None),
        P(),
        P(),
    )
    out_specs = P("tm", "tensor", None)
    return jax.shard_map(
        per_device, mesh=mesh, in_specs=in_specs, out_specs=out_specs, check_vma=False
    )
```
